512 devices in a mesh: space: 32 (over z, core), mode: 16 (over y, x).
Axes of the slice: x: 4, y: 4, z: 16, core: 2. Of those that a mesh axis runs over, the one named last changes fastest.
Arguments:
- basis: float32 [3, 256, 16, 8, 2048], P(None, 'space', None, None, 'mode'), may hold values from -132 to 132
- mean_flow: float32 [3, 256, 16, 8], P(None, 'space'), may hold values from -3 to 3
- flow_gradient: float32 [3, 3, 256, 16, 8], P(None, None, 'space'), may hold values from -2 to 2
- viscosity: float32 [256, 16, 8], P('space'), may hold values from 0.02 to 0.2
Outputs:
- reduced: float32 [2048, 2048], P('mode', 'space')
- advected: float32 [3, 256, 16, 8, 2048], P(None, 'space', None, None, 'mode')
- r_factor: float32 [2048, 128], P('mode')
The draws below stay inside these ranges and needn't reach their ends.
All inputs are finite; a program needn't handle non-finite values.
Results may differ from the reference program's by a relative error of at most 0.00074.
Values may be sent and summed in bfloat16 or wider, within the bound.
No kernel may reach another device: no remote copies, remote signals or barrier semaphores. Data moves between devices by JAX's collectives and lax.ppermute only.
A program may use at most 64 MiB of HBM per device.

```python
import math
import jax
import jax.numpy as jnp
from jax import lax

PANEL = 128
NY = 16
NZ = 8
NX = 256
MODES = 2048


def draw_basis(key, part):
    base_key = jax.random.fold_in(key, 11)
    noise_key, cell_key, mode_key = jax.random.split(base_key, 3)
    amplitude = jnp.sqrt(jnp.float32(NX) / jnp.float32(PANEL))
    cell_part = jnp.clip(jax.random.normal(cell_key, (3, NX, NY, NZ, 1), jnp.float32), -3.0, 3.0)
    mode_part = jnp.clip(jax.random.normal(mode_key, (1, NX, 1, 1, MODES), jnp.float32), -3.0, 3.0)
    noise = jnp.clip(jax.random.normal(noise_key, (3, NX, NY, NZ, MODES), jnp.float32), -6.0, 6.0)
    return noise + amplitude * cell_part * mode_part


def level_of(own_key, dims, shards, low, high):
    loudness = 1.0
    for position, shards_of in shards:
        steps = jax.random.uniform(jax.random.fold_in(jax.random.fold_in(own_key, 6), position), (shards_of,), jnp.float32, low / len(shards), high / len(shards))
        loudness = loudness * jnp.repeat(jnp.exp(steps), dims[position] // shards_of).reshape((-1,) + (1,) * (len(dims) - 1 - position))
    return loudness


def normal_values(key, extent, deviation, reach, cuts=(), held_as=jnp.bfloat16):
    values = deviation * jax.random.normal(key, extent, jnp.float32)
    if cuts:
        values = values * level_of(key, extent, cuts, -0.22, 0.18)
    return jnp.clip(values, -reach, reach).astype(held_as)


def setup_inputs(seed: int = 0) -> dict:
    keys = jax.random.split(jax.random.key(seed), 5)
    basis = draw_basis(jax.random.fold_in(keys[4], 71), 0)
    mean_flow = normal_values(keys[1], (3, NX, NY, NZ), 0.5, 3.0, ((1, 32),), jnp.float32)
    flow_gradient = normal_values(keys[2], (3, 3, NX, NY, NZ), 0.3, 2.0, ((2, 32),), jnp.float32)
    viscosity = jnp.clip(jnp.exp(math.log(0.2) - 2.3025851 * jax.random.uniform(keys[3], (NX, NY, NZ), jnp.float32) ** level_of(keys[3], (NX, NY, NZ), ((0, 32),), -0.2, 0.2)), 0.02, 0.2)
    return {"basis": basis, "mean_flow": mean_flow, "flow_gradient": flow_gradient, "viscosity": viscosity}


def transport(padded, mean_flow, flow_gradient, viscosity):
    center = padded[:, 1:-1]
    widen_y = jnp.pad(center, ((0, 0), (0, 0), (1, 1), (0, 0), (0, 0)))
    widen_z = jnp.pad(center, ((0, 0), (0, 0), (0, 0), (1, 1), (0, 0)))
    east_side = padded[:, 2:]
    west_side = padded[:, :-2]
    north_side = widen_y[:, :, 2:]
    south_side = widen_y[:, :, :-2]
    upper_side = widen_z[:, :, :, 2:]
    lower_side = widen_z[:, :, :, :-2]
    laplacian = east_side + west_side + north_side + south_side + upper_side + lower_side - 6.0 * center
    advection = 0.5 * (mean_flow[0][None, :, :, :, None] * (east_side - west_side) + mean_flow[1][None, :, :, :, None] * (north_side - south_side) + mean_flow[2][None, :, :, :, None] * (upper_side - lower_side))
    coupling = flow_gradient[:, 0][..., None] * center[0][None]
    coupling = coupling + flow_gradient[:, 1][..., None] * center[1][None]
    coupling = coupling + flow_gradient[:, 2][..., None] * center[2][None]
    return viscosity[None, :, :, :, None] * laplacian - advection - coupling

def reference(basis, mean_flow, flow_gradient, viscosity):
    panels = MODES // PANEL
    total_rows = 3 * NX * NY * NZ
    weight = 1.0 / total_rows
    stacked = basis.reshape(total_rows, panels, PANEL).transpose(1, 0, 2)
    gram = jnp.einsum('pra,prb->pab', stacked, stacked, precision=lax.Precision.HIGHEST) * weight
    lower_factor = jnp.linalg.cholesky(gram)
    solved = jax.scipy.linalg.solve_triangular(lower_factor, stacked.transpose(0, 2, 1), lower=True)
    ortho = solved.transpose(0, 2, 1)
    r_factor = lower_factor.transpose(0, 2, 1).reshape(MODES, PANEL)

    def one_panel(panel_rows):
        field = panel_rows.reshape(3, NX, NY, NZ, PANEL)
        padded = jnp.pad(field, ((0, 0), (1, 1), (0, 0), (0, 0), (0, 0)))
        image = transport(padded, mean_flow, flow_gradient, viscosity)
        return image.reshape(total_rows, PANEL)
    advected_rows = lax.map(one_panel, ortho)
    q_all = ortho.astype(jnp.bfloat16).transpose(1, 0, 2).reshape(total_rows, MODES).astype(jnp.float32)
    w_all = advected_rows.transpose(1, 0, 2).reshape(total_rows, MODES)
    w_round = w_all.astype(jnp.bfloat16).astype(jnp.float32)
    reduced = jnp.dot(q_all.T.astype(jnp.float32), w_round.astype(jnp.float32), preferred_element_type=jnp.float32) * weight
    advected = w_all.reshape(3, NX, NY, NZ, MODES)
    return (reduced, advected, r_factor)
```

```python
import functools

import jax
import jax.numpy as jnp
from jax import lax
from jax.experimental import pallas as pl
from jax.experimental.pallas import tpu as pltpu
from jax.sharding import Mesh
from jax.sharding import PartitionSpec as P

F32 = jnp.float32
BF16 = jnp.bfloat16
AXES = ("zh", "zl", "core", "y", "x")
SPACE = ("zh", "zl", "core")
MODE = ("y", "x")
VMEM_BYTES = 48 * 1024 * 1024


def kernel_call(body, outs, scratch=(), flops=0, moved=0, name=None):
    whole = pl.BlockSpec(memory_space=pltpu.VMEM)
    multiple = isinstance(outs, (tuple, list))
    return pl.pallas_call(
        body,
        out_shape=outs,
        out_specs=[whole] * len(outs) if multiple else whole,
        scratch_shapes=list(scratch),
        compiler_params=pltpu.CompilerParams(vmem_limit_bytes=VMEM_BYTES),
        cost_estimate=pl.CostEstimate(flops=flops, bytes_accessed=moved, transcendentals=0),
        name=name,
    )


def split3(a):
    high = a.astype(BF16)
    rest = a - high.astype(F32)
    mid = rest.astype(BF16)
    low = (rest - mid.astype(F32)).astype(BF16)
    return high, mid, low


def dot_rows(a, b):
    return lax.dot_general(a, b, (((0,), (0,)), ((), ())), preferred_element_type=F32)


def gram_kernel(x_ref, out_ref):
    rows = x_ref.shape[0]
    step = rows // 3
    total = jnp.zeros((256, 256), F32)
    side = jnp.zeros((128, 128), F32)
    for start in range(0, rows, step):
        high, mid, low = split3(x_ref[start : start + step, :])
        both = jnp.concatenate([high, mid], axis=1)
        total = total + dot_rows(both, both)
        side = side + dot_rows(high, low)
    gram = total[:128, :128] + total[:128, 128:] + total[128:, :128] + total[128:, 128:]
    gram = gram + side + side.T
    top, bottom = gram[:64], gram[64:]
    row = lax.broadcasted_iota(jnp.int32, (64, 128), 0)
    lane = lax.broadcasted_iota(jnp.int32, (64, 128), 1)
    packed = jnp.where((lane >= 64) & (row >= lane - 64), pltpu.roll(top, 64, 1), bottom)
    diagonal = jnp.sum(jnp.where(row == lane - 64, bottom, 0.0), axis=0, keepdims=True)
    out_ref[:64, :] = packed
    out_ref[64:, :] = jnp.broadcast_to(diagonal, (8, 128))


def stencil_kernel(x_ref, west_ref, east_ref, flow_ref, gradient_ref, viscosity_ref, out_ref):
    cells_x, cells_y = x_ref.shape[1], x_ref.shape[2]
    level = lax.broadcasted_iota(jnp.int32, (8, 128), 0)
    nu = viscosity_ref[...].T
    half = [0.5 * flow_ref[d].T for d in range(3)]
    to_east, to_west = nu - half[0], nu + half[0]
    to_north, to_south = nu - half[1], nu + half[1]
    to_upper = jnp.where(level < 7, nu - half[2], 0.0)
    to_lower = jnp.where(level > 0, nu + half[2], 0.0)
    own = [[gradient_ref[3 * i + j].T for j in range(3)] for i in range(3)]
    for i in range(3):
        own[i][i] = own[i][i] + 6.0 * nu
    for x in range(cells_x):
        for y in range(cells_y):
            place = x * cells_y + y

            def cell(values, place=place):
                return jnp.broadcast_to(values[:, place : place + 1], (8, 128))

            east_c, west_c = cell(to_east), cell(to_west)
            north_c = cell(to_north) if y + 1 < cells_y else None
            south_c = cell(to_south) if y > 0 else None
            upper_c, lower_c = cell(to_upper), cell(to_lower)
            center = [x_ref[i, x, y] for i in range(3)]
            for i in range(3):
                east = x_ref[i, x + 1, y] if x + 1 < cells_x else east_ref[i, 0, y]
                west = x_ref[i, x - 1, y] if x > 0 else west_ref[i, 0, y]
                image = east_c * east + west_c * west
                if north_c is not None:
                    image = image + north_c * x_ref[i, x, y + 1]
                if south_c is not None:
                    image = image + south_c * x_ref[i, x, y - 1]
                image = image + upper_c * pltpu.roll(center[i], 7, 0)
                image = image + lower_c * pltpu.roll(center[i], 1, 0)
                for j in range(3):
                    image = image - cell(own[i][j]) * center[j]
                out_ref[i, x, y] = image


def factor_kernel(weight, parts_ref, r_ref, inverse_ref):
    packed = parts_ref[0] + parts_ref[1] + (parts_ref[2] + parts_ref[3])
    packed = packed * weight
    top = packed[:64]
    diagonal = packed[64:65]
    turned = pltpu.roll(top, 64, 1)
    across = jnp.concatenate([top, turned], axis=0).T
    row = lax.broadcasted_iota(jnp.int32, (64, 128), 0)
    lane = lax.broadcasted_iota(jnp.int32, (64, 128), 1)
    upper_half = jnp.where((lane < 64) & (row >= lane), turned, across[64:])
    lower_half = jnp.where(
        (lane < 64) | (row < lane - 64), top, jnp.where(row > lane - 64, across[:64], diagonal)
    )
    a = [upper_half[8 * b : 8 * b + 8] for b in range(8)]
    a += [lower_half[8 * b : 8 * b + 8] for b in range(8)]
    sub = lax.broadcasted_iota(jnp.int32, (8, 128), 0)
    col = lax.broadcasted_iota(jnp.int32, (8, 128), 1)
    w = [jnp.where(sub + 8 * b == col, 1.0, 0.0).astype(F32) for b in range(16)]

    def spread_row(values, t):
        return jnp.broadcast_to(values[t : t + 1, :], (8, 128))

    def combine(columns, values):
        terms = [c * spread_row(values, t) for t, c in enumerate(columns)]
        while len(terms) > 1:
            terms = [p + q for p, q in zip(terms[::2], terms[1::2])]
        return terms[0]

    inverse_rows = []
    for k in range(16):
        r, v = a[k], w[k]
        e = {}
        for j in range(8):
            column = jnp.broadcast_to(r[:, 8 * k + j : 8 * k + j + 1], (8, 128))
            for i in range(j + 1):
                e[i, j] = spread_row(column, i)
        inv = {}
        u = {}
        for t in range(8):
            scale = lax.rsqrt(e[t, t])
            inv[t, t] = scale
            for j in range(t + 1, 8):
                u[t, j] = e[t, j] * scale
            for i in range(t + 1, 8):
                for j in range(i, 8):
                    e[i, j] = e[i, j] - u[t, i] * u[t, j]
        for t in range(8):
            for i in range(t + 1, 8):
                total = u[t, i] * inv[t, t]
                for m in range(t + 1, i):
                    total = total + u[m, i] * inv[m, t]
                inv[i, t] = -inv[i, i] * total
        columns, turned_columns = [], []
        for j in range(8):
            column = jnp.zeros((8, 128), F32)
            for i in range(j, 8):
                column = jnp.where(sub == i, inv[i, j], column)
            columns.append(column)
            column = jnp.zeros((8, 128), F32)
            for i in range(j + 1):
                column = jnp.where(sub == i, inv[j, i], column)
            turned_columns.append(column)
        upper = combine(columns, r)
        lower_inverse = combine(columns, v)
        r_ref[8 * k : 8 * k + 8, :] = jnp.where(col >= sub + 8 * k, upper, 0.0)
        inverse_rows.append(lower_inverse)
        if k < 15:
            z = combine(turned_columns, upper)
            zv = combine(turned_columns, lower_inverse)
            z_rows = [spread_row(z, t) for t in range(8)]
            zv_rows = [spread_row(zv, t) for t in range(8)]
            for b in range(k + 1, 16):
                cs = [
                    jnp.broadcast_to(a[b][:, 8 * k + j : 8 * k + j + 1], (8, 128)) for j in range(8)
                ]
                s = [c * z_rows[j] for j, c in enumerate(cs)]
                sv = [c * zv_rows[j] for j, c in enumerate(cs)]
                a[b] = a[b] - (((s[0] + s[1]) + (s[2] + s[3])) + ((s[4] + s[5]) + (s[6] + s[7])))
                w[b] = w[b] - (
                    ((sv[0] + sv[1]) + (sv[2] + sv[3])) + ((sv[4] + sv[5]) + (sv[6] + sv[7]))
                )
    r_inverse = jnp.concatenate(inverse_rows, axis=0).T
    high, mid, low = split3(r_inverse)
    inverse_ref[:, :128] = high
    inverse_ref[:, 128:256] = mid
    inverse_ref[:, 256:] = low


def apply_kernel(x_ref, image_ref, inverse_ref, rounded_ref, advected_ref, rounded_image_ref):
    rows = x_ref.shape[0]
    step = 512
    high, mid, low = (inverse_ref[:, 128 * t : 128 * t + 128] for t in range(3))
    pair = jnp.concatenate([high, mid], axis=1)
    main = jnp.concatenate([pair, pair], axis=0)
    side = jnp.concatenate([low, high], axis=0)

    def times(values):
        h, m, l = split3(values)
        first = jnp.dot(jnp.concatenate([h, m], axis=1), main, preferred_element_type=F32)
        second = jnp.dot(jnp.concatenate([h, l], axis=1), side, preferred_element_type=F32)
        return first[:, :128] + (first[:, 128:] + second)

    def chunk(n, carry):
        at = pl.ds(pl.multiple_of(n * step, step), step)
        rounded_ref[at, :] = times(x_ref[at, :]).astype(BF16)
        advected = times(image_ref[at, :])
        advected_ref[at, :] = advected
        rounded_image_ref[at, :] = advected.astype(BF16)
        return carry

    lax.fori_loop(0, rows // step, chunk, 0)


def product_kernel(place_ref, *refs):
    mode_refs, image_refs = refs[:5], refs[5:10]
    keep_ref, send_ref, total_ref = refs[10:]
    rows = mode_refs[0].shape[0]
    half = rows // 2
    for part in range(2):
        at = slice(part * half, part * half + half)
        wide = [
            jnp.concatenate([r[0][at, :], r[1][at, :], r[2][at, :], r[3 + part][...]], axis=1)
            for r in (mode_refs, image_refs)
        ]
        product = dot_rows(wide[1], wide[0])
        if part == 0:
            total_ref[...] = product
        else:
            total_ref[...] += product
    core, y, x = place_ref[0], place_ref[1], place_ref[2]
    for b, back_y in enumerate((0, 1, 3, 2)):
        panel_y = lax.rem(y + 4 - back_y, 4)
        for a, back_x in enumerate((0, 1, 3, 2)):
            piece = panel_y * 4 + lax.rem(x + 4 - back_x, 4)
            lanes = slice(128 * a, 128 * a + 128)
            mine = pl.ds(pl.multiple_of(128 * b + 64 * core, 64), 64)
            other = pl.ds(pl.multiple_of(128 * b + 64 * (1 - core), 64), 64)
            keep_ref[piece] = total_ref[mine, lanes]
            send_ref[piece] = total_ref[other, lanes]


def ring(shift):
    return [(i, (i + shift) % 4) for i in range(4)]


SWAP = [(0, 1), (1, 0)]


def spread(block, axis):
    half = block.shape[0] // 2
    up = lax.ppermute(block, axis, ring(1))
    down = lax.ppermute(block, axis, ring(3))
    far_up = lax.ppermute(up[:half], axis, ring(1))
    far_down = lax.ppermute(down[half:], axis, ring(3))
    return block, up, down, far_up, far_down


def copies(block, count):
    return jnp.broadcast_to(block[None], (count,) + block.shape)


def last_move():
    pairs = []
    for zh in range(4):
        for zl in range(4):
            for core in range(2):
                for y in range(4):
                    for x in range(4):
                        source = (((zh * 4 + zl) * 2 + core) * 4 + y) * 4 + x
                        target = (((zh * 4 + x) * 2 + core) * 4 + y) * 4 + zl
                        pairs.append((source, target))
    return pairs


def body(basis, mean_flow, flow_gradient, viscosity):
    _, cells_x, cells_y, cells_z, width = basis.shape
    rows = 3 * cells_x * cells_y * cells_z
    blocks = 32
    weight = 1.0 / (rows * blocks)
    flat = basis.reshape(rows, width)
    west = lax.ppermute(basis[:, -1:], SPACE, [(i, i + 1) for i in range(blocks - 1)])
    east = lax.ppermute(basis[:, :1], SPACE, [(i + 1, i) for i in range(blocks - 1)])

    gram = kernel_call(
        gram_kernel, jax.ShapeDtypeStruct((72, 128), F32), flops=600_000_000, moved=1_600_000
    )(flat)
    image = kernel_call(
        stencil_kernel, jax.ShapeDtypeStruct(basis.shape, F32), flops=30_000_000, moved=3_500_000
    )(
        basis,
        west,
        east,
        mean_flow.reshape(3, cells_x * cells_y, cells_z),
        flow_gradient.reshape(9, cells_x * cells_y, cells_z),
        viscosity.reshape(cells_x * cells_y, cells_z),
    ).reshape(rows, width)

    gram = gram + lax.ppermute(gram, "core", SWAP)
    gram = jnp.sum(lax.all_to_all(copies(gram, 4), "zl", 0, 0, tiled=True), axis=0)
    parts = lax.all_to_all(copies(gram, 4), "zh", 0, 0, tiled=True)
    r_factor, inverse = kernel_call(
        functools.partial(factor_kernel, weight),
        (jax.ShapeDtypeStruct((128, 128), F32), jax.ShapeDtypeStruct((128, 384), BF16)),
        flops=10_000_000,
        moved=400_000,
    )(parts)

    rounded, advected, rounded_image = kernel_call(
        apply_kernel,
        (
            jax.ShapeDtypeStruct((rows, width), BF16),
            jax.ShapeDtypeStruct((rows, width), F32),
            jax.ShapeDtypeStruct((rows, width), BF16),
        ),
        flops=1_200_000_000,
        moved=6_000_000,
    )(flat, image, inverse)

    place = jnp.stack([lax.axis_index("core"), lax.axis_index("y"), lax.axis_index("x")])
    pieces = jax.ShapeDtypeStruct((16, 64, 128), F32)
    whole = pl.BlockSpec(memory_space=pltpu.VMEM)
    keep, send = pl.pallas_call(
        product_kernel,
        out_shape=(pieces, pieces),
        in_specs=[pl.BlockSpec(memory_space=pltpu.SMEM)] + [whole] * 10,
        out_specs=[whole, whole],
        scratch_shapes=[pltpu.VMEM((512, 512), F32)],
        compiler_params=pltpu.CompilerParams(vmem_limit_bytes=VMEM_BYTES),
        cost_estimate=pl.CostEstimate(
            flops=1_600_000_000, bytes_accessed=8_000_000, transcendentals=0
        ),
    )(place, *spread(rounded, "x"), *spread(rounded_image, "y"))

    partial = keep + lax.ppermute(send, "core", SWAP)
    summands = lax.all_to_all(partial, ("zh", "zl"), 0, 0, tiled=True)
    piece = jnp.sum(summands, axis=0) * weight
    reduced = lax.ppermute(piece, AXES, last_move()).T
    return reduced, advected.reshape(basis.shape), r_factor


def solution(mesh):
    fine = Mesh(mesh.devices.reshape(4, 4, 2, 4, 4), AXES)
    placed = (
        P(None, SPACE, None, None, MODE),
        P(None, SPACE, None, None),
        P(None, None, SPACE, None, None),
        P(SPACE, None, None),
    )
    return jax.shard_map(
        body,
        mesh=fine,
        in_specs=placed,
        out_specs=(P(MODE, SPACE), P(None, SPACE, None, None, MODE), P(MODE, None)),
        check_vma=False,
    )
```

```python
import functools

import jax
import jax.numpy as jnp
from jax import lax
from jax.experimental import pallas as pl
from jax.experimental.pallas import tpu as pltpu
from jax.sharding import Mesh
from jax.sharding import PartitionSpec as P

F32 = jnp.float32
BF16 = jnp.bfloat16
AXES = ("zh", "zl", "core", "y", "x")
SPACE = ("zh", "zl", "core")
MODE = ("y", "x")
VMEM_BYTES = 16 * 1024 * 1024


def kernel_call(body, outs, scratch=(), flops=0, moved=0, name=None):
    whole = pl.BlockSpec(memory_space=pltpu.VMEM)
    multiple = isinstance(outs, (tuple, list))
    return pl.pallas_call(
        body,
        out_shape=outs,
        out_specs=[whole] * len(outs) if multiple else whole,
        scratch_shapes=list(scratch),
        compiler_params=pltpu.CompilerParams(vmem_limit_bytes=VMEM_BYTES),
        cost_estimate=pl.CostEstimate(flops=flops, bytes_accessed=moved, transcendentals=0),
        name=name,
    )


def split3(a):
    high = a.astype(BF16)
    rest = a - high.astype(F32)
    mid = rest.astype(BF16)
    low = (rest - mid.astype(F32)).astype(BF16)
    return high, mid, low


def dot_rows(a, b):
    return lax.dot_general(a, b, (((0,), (0,)), ((), ())), preferred_element_type=F32)


def coefficient_kernel(flow_ref, gradient_ref, viscosity_ref, out_ref):
    def wide(values):
        return jnp.concatenate([values[x] for x in range(values.shape[0])], axis=1)

    nu = wide(viscosity_ref[...])
    level = lax.broadcasted_iota(jnp.int32, nu.shape, 0)
    for d in range(3):
        half = 0.5 * wide(flow_ref[d])
        ahead, back = nu - half, nu + half
        if d == 2:
            ahead = jnp.where(level < nu.shape[0] - 1, ahead, 0.0)
            back = jnp.where(level > 0, back, 0.0)
        out_ref[2 * d] = ahead
        out_ref[2 * d + 1] = back
    for i in range(3):
        for j in range(3):
            own = wide(gradient_ref[i, j])
            out_ref[6 + 3 * i + j] = own + 6.0 * nu if i == j else own


def gram_kernel(x_ref, out_ref):
    rows = x_ref.shape[0]
    step = rows // 3
    total = jnp.zeros((256, 256), F32)
    side = jnp.zeros((128, 128), F32)
    for start in range(0, rows, step):
        high, mid, low = split3(x_ref[start : start + step, :])
        both = jnp.concatenate([high, mid], axis=1)
        total = total + dot_rows(both, both)
        side = side + dot_rows(high, low)
    gram = total[:128, :128] + total[:128, 128:] + total[128:, :128] + total[128:, 128:]
    gram = gram + side + side.T
    top, bottom = gram[:64], gram[64:]
    row = lax.broadcasted_iota(jnp.int32, (64, 128), 0)
    lane = lax.broadcasted_iota(jnp.int32, (64, 128), 1)
    packed = jnp.where((lane >= 64) & (row >= lane - 64), pltpu.roll(top, 64, 1), bottom)
    diagonal = jnp.sum(jnp.where(row == lane - 64, bottom, 0.0), axis=0, keepdims=True)
    out_ref[:64, :] = packed
    out_ref[64:, :] = jnp.broadcast_to(diagonal, (8, 128))


def times_inverse(inverse):
    high, mid, low = (inverse[:, 128 * t : 128 * t + 128] for t in range(3))
    pair = jnp.concatenate([high, mid], axis=1)
    main = jnp.concatenate([pair, pair], axis=0)
    side = jnp.concatenate([low, high], axis=0)

    def times(values):
        h, m, l = split3(values)
        first = jnp.dot(jnp.concatenate([h, m], axis=1), main, preferred_element_type=F32)
        second = jnp.dot(jnp.concatenate([h, l], axis=1), side, preferred_element_type=F32)
        return first[:, :128] + (first[:, 128:] + second)

    return times


def modes_kernel(x_ref, inverse_ref, rounded_ref):
    times = times_inverse(inverse_ref[...])
    step = 1024
    for first in range(0, x_ref.shape[0], step):
        at = slice(first, first + step)
        rounded_ref[at, :] = times(x_ref[at, :]).astype(BF16)


def image_kernel(
    x_ref, west_ref, east_ref, coefficient_ref, inverse_ref,
    advected_ref, rounded_ref, raw_ref, sems,
):
    cells_x, cells_y, cells_z = x_ref.shape[1:4]
    layer = cells_y * cells_z
    times = times_inverse(inverse_ref[...])
    sent = []
    values = [coefficient_ref[n] for n in range(15)]
    for x in range(cells_x):
        for y in range(cells_y):
            place = slice(x * cells_y + y, x * cells_y + y + 1)
            cell = [jnp.broadcast_to(v[:, place], (8, 128)) for v in values]
            east_c, west_c, north_c, south_c, upper_c, lower_c = cell[:6]
            center = [x_ref[i, x, y] for i in range(3)]
            for i in range(3):
                east = x_ref[i, x + 1, y] if x + 1 < cells_x else east_ref[i, 0, y]
                west = x_ref[i, x - 1, y] if x > 0 else west_ref[i, 0, y]
                image = east_c * east + west_c * west
                if y + 1 < cells_y:
                    image = image + north_c * x_ref[i, x, y + 1]
                if y > 0:
                    image = image + south_c * x_ref[i, x, y - 1]
                image = image + upper_c * pltpu.roll(center[i], 7, 0)
                image = image + lower_c * pltpu.roll(center[i], 1, 0)
                for j in range(3):
                    image = image - cell[6 + 3 * i + j] * center[j]
                first = ((i * cells_x + x) * cells_y + y) * cells_z
                raw_ref[first : first + cells_z, :] = image

        if x % 2 == 1:
            for i in range(3):
                first = (i * cells_x + x - 1) * layer
                at = pl.ds(first, 2 * layer)
                advected = times(raw_ref[at, :])
                raw_ref[at, :] = advected
                rounded_ref[at, :] = advected.astype(BF16)
                sent.append(
                    pltpu.make_async_copy(
                        raw_ref.at[at, :], advected_ref.at[at, :], sems.at[len(sent)]
                    )
                )
                sent[-1].start()
    for copy in sent:
        copy.wait()


def pair_kernel(a_ref, b_ref, out_ref):
    total = a_ref[...] + b_ref[...]
    for n in range(4):
        out_ref[n] = total


def four_kernel(parts_ref, out_ref):
    total = (parts_ref[0] + parts_ref[1]) + (parts_ref[2] + parts_ref[3])
    for n in range(4):
        out_ref[n] = total


def factor_kernel(weight, parts_ref, west_ref, east_ref, coefficient_ref, r_ref, inverse_ref):
    del west_ref, east_ref, coefficient_ref
    packed = parts_ref[0] + parts_ref[1] + (parts_ref[2] + parts_ref[3])
    packed = packed * weight
    top = packed[:64]
    diagonal = packed[64:65]
    turned = pltpu.roll(top, 64, 1)
    across = jnp.concatenate([top, turned], axis=0).T
    row = lax.broadcasted_iota(jnp.int32, (64, 128), 0)
    lane = lax.broadcasted_iota(jnp.int32, (64, 128), 1)
    upper_half = jnp.where((lane < 64) & (row >= lane), turned, across[64:])
    lower_half = jnp.where(
        (lane < 64) | (row < lane - 64), top, jnp.where(row > lane - 64, across[:64], diagonal)
    )
    a = [upper_half[8 * b : 8 * b + 8] for b in range(8)]
    a += [lower_half[8 * b : 8 * b + 8] for b in range(8)]
    sub = lax.broadcasted_iota(jnp.int32, (8, 128), 0)
    col = lax.broadcasted_iota(jnp.int32, (8, 128), 1)
    w = [jnp.where(sub + 8 * b == col, 1.0, 0.0).astype(F32) for b in range(16)]

    def spread_row(values, t):
        return jnp.broadcast_to(values[t : t + 1, :], (8, 128))

    def combine(columns, values):
        terms = [c * spread_row(values, t) for t, c in enumerate(columns)]
        while len(terms) > 1:
            terms = [p + q for p, q in zip(terms[::2], terms[1::2])]
        return terms[0]

    inverse_rows = []
    for k in range(16):
        r, v = a[k], w[k]
        e = {}
        for j in range(8):
            column = jnp.broadcast_to(r[:, 8 * k + j : 8 * k + j + 1], (8, 128))
            for i in range(j + 1):
                e[i, j] = spread_row(column, i)
        inv = {}
        u = {}
        for t in range(8):
            scale = lax.rsqrt(e[t, t])
            inv[t, t] = scale
            for j in range(t + 1, 8):
                u[t, j] = e[t, j] * scale
            for i in range(t + 1, 8):
                for j in range(i, 8):
                    e[i, j] = e[i, j] - u[t, i] * u[t, j]
        for t in range(8):
            for i in range(t + 1, 8):
                total = u[t, i] * inv[t, t]
                for m in range(t + 1, i):
                    total = total + u[m, i] * inv[m, t]
                inv[i, t] = -inv[i, i] * total
        columns, turned_columns = [], []
        for j in range(8):
            column = jnp.zeros((8, 128), F32)
            for i in range(j, 8):
                column = jnp.where(sub == i, inv[i, j], column)
            columns.append(column)
            column = jnp.zeros((8, 128), F32)
            for i in range(j + 1):
                column = jnp.where(sub == i, inv[j, i], column)
            turned_columns.append(column)
        upper = combine(columns, r)
        lower_inverse = combine(columns, v)
        r_ref[8 * k : 8 * k + 8, :] = jnp.where(col >= sub + 8 * k, upper, 0.0)
        inverse_rows.append(lower_inverse)
        if k < 15:
            z = combine(turned_columns, upper)
            zv = combine(turned_columns, lower_inverse)
            z_rows = [spread_row(z, t) for t in range(8)]
            zv_rows = [spread_row(zv, t) for t in range(8)]
            for b in range(k + 1, 16):
                cs = [
                    jnp.broadcast_to(a[b][:, 8 * k + j : 8 * k + j + 1], (8, 128)) for j in range(8)
                ]
                s = [c * z_rows[j] for j, c in enumerate(cs)]
                sv = [c * zv_rows[j] for j, c in enumerate(cs)]
                a[b] = a[b] - (((s[0] + s[1]) + (s[2] + s[3])) + ((s[4] + s[5]) + (s[6] + s[7])))
                w[b] = w[b] - (
                    ((sv[0] + sv[1]) + (sv[2] + sv[3])) + ((sv[4] + sv[5]) + (sv[6] + sv[7]))
                )
    r_inverse = jnp.concatenate(inverse_rows, axis=0).T
    high, mid, low = split3(r_inverse)
    inverse_ref[:, :128] = high
    inverse_ref[:, 128:256] = mid
    inverse_ref[:, 256:] = low


def product_kernel(mode_turns, place_ref, *refs):
    mode_refs = refs[: len(mode_turns)]
    image_refs = refs[len(mode_turns) : -3]
    keep_ref, send_ref, total_ref = refs[-3:]
    half = mode_refs[0].shape[0] // 2
    for part in range(2):
        at = slice(part * half, part * half + half)
        wide = [
            jnp.concatenate([r[at, :] for r in group], axis=1) for group in (mode_refs, image_refs)
        ]
        product = dot_rows(wide[1], wide[0])
        if part == 0:
            total_ref[...] = product
        else:
            total_ref[...] += product
    core, x = place_ref[0], place_ref[1]
    ahead = 2 * core - 1
    for a, mode_turn in enumerate(mode_turns):
        panel_x = lax.rem(x + 4 + ahead * mode_turn, 4)
        lanes = slice(128 * a, 128 * a + 128)
        for b in range(len(image_refs)):
            slot = b if b == 0 else b + core * (3 - 2 * b)
            mine = pl.ds(pl.multiple_of(128 * b + 64 * core, 64), 64)
            other = pl.ds(pl.multiple_of(128 * b + 64 * (1 - core), 64), 64)
            keep_ref[panel_x, slot] = total_ref[mine, lanes]
            send_ref[panel_x, slot] = total_ref[other, lanes]


def product(place, modes, images, mode_turns):
    shape = jax.ShapeDtypeStruct((4, len(images), 64, 128), F32)
    whole = pl.BlockSpec(memory_space=pltpu.VMEM)
    return pl.pallas_call(
        functools.partial(product_kernel, mode_turns),
        out_shape=(shape, shape),
        in_specs=[pl.BlockSpec(memory_space=pltpu.SMEM)] + [whole] * (len(modes) + len(images)),
        out_specs=[whole, whole],
        scratch_shapes=[pltpu.VMEM((128 * len(images), 128 * len(modes)), F32)],
        compiler_params=pltpu.CompilerParams(vmem_limit_bytes=VMEM_BYTES),
        cost_estimate=pl.CostEstimate(
            flops=100_000_000 * len(modes) * len(images), bytes_accessed=6_000_000, transcendentals=0
        ),
    )(place, *modes, *images)


def join_kernel(keep_ref, received_ref, keep_last_ref, received_last_ref, out_ref):
    for n in range(4):
        out_ref[n, :3] = keep_ref[n] + received_ref[n]
        out_ref[n, 3] = keep_last_ref[n, 0] + received_last_ref[n, 0]


def near_kernel(place_ref, parts_ref, out_ref):
    y = place_ref[2]
    for slot, turn in enumerate((0, -1, 1, 2)):
        out_ref[lax.rem(y + 4 + turn, 4)] = (parts_ref[0, slot] + parts_ref[1, slot]) + (
            parts_ref[2, slot] + parts_ref[3, slot]
        )


def far_kernel(weight, parts_ref, out_ref):
    out_ref[...] = ((parts_ref[0] + parts_ref[1]) + (parts_ref[2] + parts_ref[3])) * weight


AHEAD = [(i, (i + 1) % 4) for i in range(4)] + [(4 + i, 4 + (i + 3) % 4) for i in range(4)]
BACK = [(target, source) for source, target in AHEAD]


def pass_on(block, axis, pairs):
    return lax.ppermute(block, ("core", axis), pairs)


SWAP = [(0, 1), (1, 0)]


def copies(block, count):
    return jnp.broadcast_to(block[None], (count,) + block.shape)


def turn_over(block):
    pairs = [(4 * zl + x, 4 * x + zl) for zl in range(4) for x in range(4)]
    return lax.ppermute(block, ("zl", "x"), pairs)


def body(basis, mean_flow, flow_gradient, viscosity):
    _, cells_x, cells_y, cells_z, width = basis.shape
    rows = 3 * cells_x * cells_y * cells_z
    blocks = 32
    weight = 1.0 / (rows * blocks)
    flat = basis.reshape(rows, width)
    west = lax.ppermute(basis[:, -1:], SPACE, [(i, i + 1) for i in range(blocks - 1)])
    east = lax.ppermute(basis[:, :1], SPACE, [(i + 1, i) for i in range(blocks - 1)])

    packed = jax.ShapeDtypeStruct((72, 128), F32)
    packed4 = jax.ShapeDtypeStruct((4, 72, 128), F32)
    gram = kernel_call(gram_kernel, packed, flops=600_000_000, moved=1_600_000)(flat)
    coefficients = kernel_call(
        coefficient_kernel,
        jax.ShapeDtypeStruct((15, cells_z, cells_x * cells_y), F32),
        flops=200_000,
        moved=500_000,
    )(mean_flow.swapaxes(2, 3), flow_gradient.swapaxes(3, 4), viscosity.swapaxes(1, 2))
    received = lax.ppermute(gram, "core", SWAP)
    mine = kernel_call(pair_kernel, packed4, moved=200_000)(gram, received)
    near = lax.all_to_all(mine, "zl", 0, 0, tiled=True)
    near = kernel_call(four_kernel, packed4, moved=300_000)(near)
    parts = lax.all_to_all(near, "zh", 0, 0, tiled=True)
    whole = pl.BlockSpec(memory_space=pltpu.VMEM)
    anywhere = pl.BlockSpec(memory_space=pl.ANY)
    r_factor, inverse = pl.pallas_call(
        functools.partial(factor_kernel, weight),
        out_shape=(
            jax.ShapeDtypeStruct((128, 128), F32),
            jax.ShapeDtypeStruct((128, 384), BF16),
        ),
        in_specs=[whole, anywhere, anywhere, anywhere],
        out_specs=[whole, whole],
        compiler_params=pltpu.CompilerParams(vmem_limit_bytes=VMEM_BYTES),
        cost_estimate=pl.CostEstimate(flops=10_000_000, bytes_accessed=400_000, transcendentals=0),
    )(parts, west, east, coefficients)
    rounded = pl.pallas_call(
        modes_kernel,
        out_shape=jax.ShapeDtypeStruct((rows, width), BF16),
        in_specs=[whole, whole],
        out_specs=whole,
        compiler_params=pltpu.CompilerParams(vmem_limit_bytes=VMEM_BYTES),
        cost_estimate=pl.CostEstimate(
            flops=600_000_000, bytes_accessed=2_400_000, transcendentals=0
        ),
    )(flat, inverse)
    modes = [rounded, pass_on(rounded, "x", AHEAD), pass_on(rounded, "x", BACK)]
    advected, rounded_image = pl.pallas_call(
        image_kernel,
        out_shape=(
            jax.ShapeDtypeStruct((rows, width), F32),
            jax.ShapeDtypeStruct((rows, width), BF16),
        ),
        in_specs=[whole] * 5,
        out_specs=[anywhere, whole],
        scratch_shapes=[
            pltpu.VMEM((rows, width), F32),
            pltpu.SemaphoreType.DMA((3 * (cells_x // 2),)),
        ],
        compiler_params=pltpu.CompilerParams(vmem_limit_bytes=VMEM_BYTES),
        cost_estimate=pl.CostEstimate(
            flops=600_000_000, bytes_accessed=5_000_000, transcendentals=0
        ),
    )(
        basis,
        west,
        east,
        coefficients,
        inverse,
    )
    images = [rounded_image, pass_on(rounded_image, "y", AHEAD), pass_on(rounded_image, "y", BACK)]
    modes.append(pass_on(modes[1], "x", AHEAD))
    last_image = pass_on(images[1], "y", AHEAD)

    place = jnp.stack([lax.axis_index(axis) for axis in ("core", "x", "y")])
    turns = (0, 1, -1, 2)
    keep, send = product(place, modes, images, turns)
    received = lax.ppermute(send, "core", SWAP)
    keep_last, send_last = product(place, modes, [last_image], turns)
    received_last = lax.ppermute(send_last, "core", SWAP)
    partial = kernel_call(
        join_kernel, jax.ShapeDtypeStruct((4, 4, 64, 128), F32), moved=1_500_000
    )(keep, received, keep_last, received_last)
    near = lax.all_to_all(partial, "zl", 0, 0, tiled=True)
    near = pl.pallas_call(
        near_kernel,
        out_shape=jax.ShapeDtypeStruct((4, 64, 128), F32),
        in_specs=[pl.BlockSpec(memory_space=pltpu.SMEM), whole],
        out_specs=whole,
        compiler_params=pltpu.CompilerParams(vmem_limit_bytes=VMEM_BYTES),
    )(place, near)
    far = lax.all_to_all(near, "zh", 0, 0, tiled=True)
    piece = kernel_call(
        functools.partial(far_kernel, weight), jax.ShapeDtypeStruct((64, 128), F32), moved=200_000
    )(far)
    reduced = turn_over(piece).T
    return reduced, advected.reshape(basis.shape), r_factor


def solution(mesh):
    fine = Mesh(mesh.devices.reshape(4, 4, 2, 4, 4), AXES)
    placed = (
        P(None, SPACE, None, None, MODE),
        P(None, SPACE, None, None),
        P(None, None, SPACE, None, None),
        P(SPACE, None, None),
    )
    return jax.shard_map(
        body,
        mesh=fine,
        in_specs=placed,
        out_specs=(P(MODE, SPACE), P(None, SPACE, None, None, MODE), P(MODE, None)),
        check_vma=False,
    )
```

```python
import functools

import jax
import jax.numpy as jnp
from jax import lax
from jax.experimental import pallas as pl
from jax.experimental.pallas import tpu as pltpu
from jax.sharding import Mesh
from jax.sharding import PartitionSpec as P

F32 = jnp.float32
BF16 = jnp.bfloat16
AXES = ("zh", "zl", "core", "y", "x")
SPACE = ("zh", "zl", "core")
MODE = ("y", "x")
VMEM_BYTES = 16 * 1024 * 1024


def kernel_call(body, outs, scratch=(), flops=0, moved=0, name=None):
    whole = pl.BlockSpec(memory_space=pltpu.VMEM)
    multiple = isinstance(outs, (tuple, list))
    return pl.pallas_call(
        body,
        out_shape=outs,
        out_specs=[whole] * len(outs) if multiple else whole,
        scratch_shapes=list(scratch),
        compiler_params=pltpu.CompilerParams(vmem_limit_bytes=VMEM_BYTES),
        cost_estimate=pl.CostEstimate(flops=flops, bytes_accessed=moved, transcendentals=0),
        name=name,
    )


def split3(a):
    high = a.astype(BF16)
    rest = a - high.astype(F32)
    mid = rest.astype(BF16)
    low = (rest - mid.astype(F32)).astype(BF16)
    return high, mid, low


def dot_rows(a, b):
    return lax.dot_general(a, b, (((0,), (0,)), ((), ())), preferred_element_type=F32)


def coefficient_kernel(flow_ref, gradient_ref, viscosity_ref, out_ref):
    def wide(values):
        return jnp.concatenate([values[x] for x in range(values.shape[0])], axis=1)

    nu = wide(viscosity_ref[...])
    level = lax.broadcasted_iota(jnp.int32, nu.shape, 0)
    for d in range(3):
        half = 0.5 * wide(flow_ref[d])
        ahead, back = nu - half, nu + half
        if d == 2:
            ahead = jnp.where(level < nu.shape[0] - 1, ahead, 0.0)
            back = jnp.where(level > 0, back, 0.0)
        out_ref[2 * d] = ahead
        out_ref[2 * d + 1] = back
    for i in range(3):
        for j in range(3):
            own = wide(gradient_ref[i, j])
            out_ref[6 + 3 * i + j] = own + 6.0 * nu if i == j else own


def gram_kernel(x_ref, out_ref):
    rows = x_ref.shape[0]
    step = rows // 3
    total = jnp.zeros((256, 256), F32)
    side = jnp.zeros((128, 128), F32)
    for start in range(0, rows, step):
        high, mid, low = split3(x_ref[start : start + step, :])
        both = jnp.concatenate([high, mid], axis=1)
        total = total + dot_rows(both, both)
        side = side + dot_rows(high, low)
    gram = total[:128, :128] + total[:128, 128:] + total[128:, :128] + total[128:, 128:]
    gram = gram + side + side.T
    top, bottom = gram[:64], gram[64:]
    row = lax.broadcasted_iota(jnp.int32, (64, 128), 0)
    lane = lax.broadcasted_iota(jnp.int32, (64, 128), 1)
    packed = jnp.where((lane >= 64) & (row >= lane - 64), pltpu.roll(top, 64, 1), bottom)
    diagonal = jnp.sum(jnp.where(row == lane - 64, bottom, 0.0), axis=0, keepdims=True)
    out_ref[:64, :] = packed
    out_ref[64:, :] = jnp.broadcast_to(diagonal, (8, 128))


def times_inverse(inverse):
    high, mid, low = (inverse[:, 128 * t : 128 * t + 128] for t in range(3))
    pair = jnp.concatenate([high, mid], axis=1)
    main = jnp.concatenate([pair, pair], axis=0)
    side = jnp.concatenate([low, high], axis=0)

    def times(values):
        h, m, l = split3(values)
        first = jnp.dot(jnp.concatenate([h, m], axis=1), main, preferred_element_type=F32)
        second = jnp.dot(jnp.concatenate([h, l], axis=1), side, preferred_element_type=F32)
        return first[:, :128] + (first[:, 128:] + second)

    return times


def modes_kernel(x_ref, inverse_ref, rounded_ref):
    times = times_inverse(inverse_ref[...])
    step = 1024
    for first in range(0, x_ref.shape[0], step):
        at = slice(first, first + step)
        rounded_ref[at, :] = times(x_ref[at, :]).astype(BF16)


def image_layer(x, x_ref, beside, coefficient_ref, out_ref):
    cells_x, cells_y, cells_z = x_ref.shape[1:4]
    values = [coefficient_ref[n] for n in range(15)]
    for y in range(cells_y):
        place = slice(x * cells_y + y, x * cells_y + y + 1)
        cell = [jnp.broadcast_to(v[:, place], (8, 128)) for v in values]
        east_c, west_c, north_c, south_c, upper_c, lower_c = cell[:6]
        center = [x_ref[i, x, y] for i in range(3)]
        for i in range(3):
            image = east_c * beside(i, x + 1, y) + west_c * beside(i, x - 1, y)
            if y + 1 < cells_y:
                image = image + north_c * x_ref[i, x, y + 1]
            if y > 0:
                image = image + south_c * x_ref[i, x, y - 1]
            image = image + upper_c * pltpu.roll(center[i], 7, 0)
            image = image + lower_c * pltpu.roll(center[i], 1, 0)
            for j in range(3):
                image = image - cell[6 + 3 * i + j] * center[j]
            first = ((i * cells_x + x) * cells_y + y) * cells_z
            out_ref[first : first + cells_z, :] = image


def inner_kernel(x_ref, coefficient_ref, raw_ref):
    for x in range(1, x_ref.shape[1] - 1):
        image_layer(x, x_ref, lambda i, x, y: x_ref[i, x, y], coefficient_ref, raw_ref)


def image_kernel(
    x_ref, west_ref, east_ref, coefficient_ref, inner_ref, inverse_ref,
    advected_ref, rounded_ref, work_ref, sems,
):
    cells_x, cells_y, cells_z = x_ref.shape[1:4]
    layer = cells_y * cells_z

    def beside(i, x, y):
        if x < 0:
            return west_ref[i, 0, y]
        return x_ref[i, x, y] if x < cells_x else east_ref[i, 0, y]

    times = times_inverse(inverse_ref[...])
    sent = []

    def finish(source_ref, x, layers):
        for i in range(3):
            at = pl.ds((i * cells_x + x) * layer, layers * layer)
            advected = times(source_ref[at, :])
            work_ref[at, :] = advected
            rounded_ref[at, :] = advected.astype(BF16)
            sent.append(
                pltpu.make_async_copy(work_ref.at[at, :], advected_ref.at[at, :], sems.at[len(sent)])
            )
            sent[-1].start()

    half = cells_x // 2
    finish(inner_ref, 1, half - 1)
    image_layer(0, x_ref, beside, coefficient_ref, work_ref)
    finish(inner_ref, half, half - 1)
    image_layer(cells_x - 1, x_ref, beside, coefficient_ref, work_ref)
    finish(work_ref, 0, 1)
    finish(work_ref, cells_x - 1, 1)
    for copy in sent:
        copy.wait()


def pair_kernel(a_ref, b_ref, out_ref):
    total = a_ref[...] + b_ref[...]
    for n in range(4):
        out_ref[n] = total


def four_kernel(parts_ref, out_ref):
    total = (parts_ref[0] + parts_ref[1]) + (parts_ref[2] + parts_ref[3])
    for n in range(4):
        out_ref[n] = total


def factor_kernel(weight, parts_ref, west_ref, east_ref, inner_ref, r_ref, inverse_ref):
    del west_ref, east_ref, inner_ref
    packed = parts_ref[0] + parts_ref[1] + (parts_ref[2] + parts_ref[3])
    packed = packed * weight
    top = packed[:64]
    diagonal = packed[64:65]
    turned = pltpu.roll(top, 64, 1)
    across = jnp.concatenate([top, turned], axis=0).T
    row = lax.broadcasted_iota(jnp.int32, (64, 128), 0)
    lane = lax.broadcasted_iota(jnp.int32, (64, 128), 1)
    upper_half = jnp.where((lane < 64) & (row >= lane), turned, across[64:])
    lower_half = jnp.where(
        (lane < 64) | (row < lane - 64), top, jnp.where(row > lane - 64, across[:64], diagonal)
    )
    a = [upper_half[8 * b : 8 * b + 8] for b in range(8)]
    a += [lower_half[8 * b : 8 * b + 8] for b in range(8)]
    sub = lax.broadcasted_iota(jnp.int32, (8, 128), 0)
    col = lax.broadcasted_iota(jnp.int32, (8, 128), 1)
    w = [jnp.where(sub + 8 * b == col, 1.0, 0.0).astype(F32) for b in range(16)]

    def spread_row(values, t):
        return jnp.broadcast_to(values[t : t + 1, :], (8, 128))

    def combine(columns, values):
        terms = [c * spread_row(values, t) for t, c in enumerate(columns)]
        while len(terms) > 1:
            terms = [p + q for p, q in zip(terms[::2], terms[1::2])]
        return terms[0]

    inverse_rows = []
    for k in range(16):
        r, v = a[k], w[k]
        e = {}
        for j in range(8):
            column = jnp.broadcast_to(r[:, 8 * k + j : 8 * k + j + 1], (8, 128))
            for i in range(j + 1):
                e[i, j] = spread_row(column, i)
        inv = {}
        u = {}
        for t in range(8):
            scale = lax.rsqrt(e[t, t])
            inv[t, t] = scale
            for j in range(t + 1, 8):
                u[t, j] = e[t, j] * scale
            for i in range(t + 1, 8):
                for j in range(i, 8):
                    e[i, j] = e[i, j] - u[t, i] * u[t, j]
        for t in range(8):
            for i in range(t + 1, 8):
                total = u[t, i] * inv[t, t]
                for m in range(t + 1, i):
                    total = total + u[m, i] * inv[m, t]
                inv[i, t] = -inv[i, i] * total
        columns, turned_columns = [], []
        for j in range(8):
            column = jnp.zeros((8, 128), F32)
            for i in range(j, 8):
                column = jnp.where(sub == i, inv[i, j], column)
            columns.append(column)
            column = jnp.zeros((8, 128), F32)
            for i in range(j + 1):
                column = jnp.where(sub == i, inv[j, i], column)
            turned_columns.append(column)
        upper = combine(columns, r)
        lower_inverse = combine(columns, v)
        r_ref[8 * k : 8 * k + 8, :] = jnp.where(col >= sub + 8 * k, upper, 0.0)
        inverse_rows.append(lower_inverse)
        if k < 15:
            z = combine(turned_columns, upper)
            zv = combine(turned_columns, lower_inverse)
            z_rows = [spread_row(z, t) for t in range(8)]
            zv_rows = [spread_row(zv, t) for t in range(8)]
            for b in range(k + 1, 16):
                cs = [
                    jnp.broadcast_to(a[b][:, 8 * k + j : 8 * k + j + 1], (8, 128)) for j in range(8)
                ]
                s = [c * z_rows[j] for j, c in enumerate(cs)]
                sv = [c * zv_rows[j] for j, c in enumerate(cs)]
                a[b] = a[b] - (((s[0] + s[1]) + (s[2] + s[3])) + ((s[4] + s[5]) + (s[6] + s[7])))
                w[b] = w[b] - (
                    ((sv[0] + sv[1]) + (sv[2] + sv[3])) + ((sv[4] + sv[5]) + (sv[6] + sv[7]))
                )
    r_inverse = jnp.concatenate(inverse_rows, axis=0).T
    high, mid, low = split3(r_inverse)
    inverse_ref[:, :128] = high
    inverse_ref[:, 128:256] = mid
    inverse_ref[:, 256:] = low


def product_kernel(mode_turns, place_ref, *refs):
    mode_refs = refs[: len(mode_turns)]
    image_refs = refs[len(mode_turns) : -3]
    keep_ref, send_ref, total_ref = refs[-3:]
    half = mode_refs[0].shape[0] // 2
    for part in range(2):
        at = slice(part * half, part * half + half)
        wide = [
            jnp.concatenate([r[at, :] for r in group], axis=1) for group in (mode_refs, image_refs)
        ]
        product = dot_rows(wide[1], wide[0])
        if part == 0:
            total_ref[...] = product
        else:
            total_ref[...] += product
    core, x = place_ref[0], place_ref[1]
    ahead = 2 * core - 1
    for a, mode_turn in enumerate(mode_turns):
        panel_x = lax.rem(x + 4 + ahead * mode_turn, 4)
        lanes = slice(128 * a, 128 * a + 128)
        for b in range(len(image_refs)):
            slot = b if b == 0 else b + core * (3 - 2 * b)
            mine = pl.ds(pl.multiple_of(128 * b + 64 * core, 64), 64)
            other = pl.ds(pl.multiple_of(128 * b + 64 * (1 - core), 64), 64)
            keep_ref[panel_x, slot] = total_ref[mine, lanes]
            send_ref[panel_x, slot] = total_ref[other, lanes]


def product(place, modes, images, mode_turns):
    shape = jax.ShapeDtypeStruct((4, len(images), 64, 128), F32)
    whole = pl.BlockSpec(memory_space=pltpu.VMEM)
    return pl.pallas_call(
        functools.partial(product_kernel, mode_turns),
        out_shape=(shape, shape),
        in_specs=[pl.BlockSpec(memory_space=pltpu.SMEM)] + [whole] * (len(modes) + len(images)),
        out_specs=[whole, whole],
        scratch_shapes=[pltpu.VMEM((128 * len(images), 128 * len(modes)), F32)],
        compiler_params=pltpu.CompilerParams(vmem_limit_bytes=VMEM_BYTES),
        cost_estimate=pl.CostEstimate(
            flops=100_000_000 * len(modes) * len(images), bytes_accessed=6_000_000, transcendentals=0
        ),
    )(place, *modes, *images)


def join_kernel(keep_ref, received_ref, keep_last_ref, received_last_ref, out_ref):
    for n in range(4):
        out_ref[n, :3] = keep_ref[n] + received_ref[n]
        out_ref[n, 3] = keep_last_ref[n, 0] + received_last_ref[n, 0]


def near_kernel(place_ref, parts_ref, out_ref):
    y = place_ref[2]
    for slot, turn in enumerate((0, -1, 1, 2)):
        out_ref[lax.rem(y + 4 + turn, 4)] = (parts_ref[0, slot] + parts_ref[1, slot]) + (
            parts_ref[2, slot] + parts_ref[3, slot]
        )


def far_kernel(weight, parts_ref, out_ref):
    out_ref[...] = ((parts_ref[0] + parts_ref[1]) + (parts_ref[2] + parts_ref[3])) * weight


AHEAD = [(i, (i + 1) % 4) for i in range(4)] + [(4 + i, 4 + (i + 3) % 4) for i in range(4)]
BACK = [(target, source) for source, target in AHEAD]


def pass_on(block, axis, pairs):
    return lax.ppermute(block, ("core", axis), pairs)


SWAP = [(0, 1), (1, 0)]


def copies(block, count):
    return jnp.broadcast_to(block[None], (count,) + block.shape)


def turn_over(block):
    pairs = [(4 * zl + x, 4 * x + zl) for zl in range(4) for x in range(4)]
    return lax.ppermute(block, ("zl", "x"), pairs)


def body(basis, mean_flow, flow_gradient, viscosity):
    _, cells_x, cells_y, cells_z, width = basis.shape
    rows = 3 * cells_x * cells_y * cells_z
    blocks = 32
    weight = 1.0 / (rows * blocks)
    flat = basis.reshape(rows, width)
    west = lax.ppermute(basis[:, -1:], SPACE, [(i, i + 1) for i in range(blocks - 1)])
    east = lax.ppermute(basis[:, :1], SPACE, [(i + 1, i) for i in range(blocks - 1)])

    packed = jax.ShapeDtypeStruct((72, 128), F32)
    packed4 = jax.ShapeDtypeStruct((4, 72, 128), F32)
    gram = kernel_call(gram_kernel, packed, flops=600_000_000, moved=1_600_000)(flat)
    coefficients = kernel_call(
        coefficient_kernel,
        jax.ShapeDtypeStruct((15, cells_z, cells_x * cells_y), F32),
        flops=200_000,
        moved=500_000,
    )(mean_flow.swapaxes(2, 3), flow_gradient.swapaxes(3, 4), viscosity.swapaxes(1, 2))
    inner = kernel_call(
        inner_kernel, jax.ShapeDtypeStruct((rows, width), F32), flops=25_000_000, moved=3_000_000
    )(basis, coefficients)
    received = lax.ppermute(gram, "core", SWAP)
    mine = kernel_call(pair_kernel, packed4, moved=200_000)(gram, received)
    near = lax.all_to_all(mine, "zl", 0, 0, tiled=True)
    near = kernel_call(four_kernel, packed4, moved=300_000)(near)
    parts = lax.all_to_all(near, "zh", 0, 0, tiled=True)
    whole = pl.BlockSpec(memory_space=pltpu.VMEM)
    anywhere = pl.BlockSpec(memory_space=pl.ANY)
    r_factor, inverse = pl.pallas_call(
        functools.partial(factor_kernel, weight),
        out_shape=(
            jax.ShapeDtypeStruct((128, 128), F32),
            jax.ShapeDtypeStruct((128, 384), BF16),
        ),
        in_specs=[whole, anywhere, anywhere, anywhere],
        out_specs=[whole, whole],
        compiler_params=pltpu.CompilerParams(vmem_limit_bytes=VMEM_BYTES),
        cost_estimate=pl.CostEstimate(flops=10_000_000, bytes_accessed=400_000, transcendentals=0),
    )(parts, west, east, inner)
    rounded = pl.pallas_call(
        modes_kernel,
        out_shape=jax.ShapeDtypeStruct((rows, width), BF16),
        in_specs=[whole, whole],
        out_specs=whole,
        compiler_params=pltpu.CompilerParams(vmem_limit_bytes=VMEM_BYTES),
        cost_estimate=pl.CostEstimate(
            flops=600_000_000, bytes_accessed=2_400_000, transcendentals=0
        ),
    )(flat, inverse)
    modes = [rounded, pass_on(rounded, "x", AHEAD), pass_on(rounded, "x", BACK)]
    advected, rounded_image = pl.pallas_call(
        image_kernel,
        out_shape=(
            jax.ShapeDtypeStruct((rows, width), F32),
            jax.ShapeDtypeStruct((rows, width), BF16),
        ),
        in_specs=[whole] * 6,
        out_specs=[anywhere, whole],
        scratch_shapes=[
            pltpu.VMEM((rows, width), F32),
            pltpu.SemaphoreType.DMA((12,)),
        ],
        compiler_params=pltpu.CompilerParams(vmem_limit_bytes=VMEM_BYTES),
        cost_estimate=pl.CostEstimate(
            flops=600_000_000, bytes_accessed=5_000_000, transcendentals=0
        ),
    )(
        basis,
        west,
        east,
        coefficients,
        inner,
        inverse,
    )
    images = [rounded_image, pass_on(rounded_image, "y", AHEAD), pass_on(rounded_image, "y", BACK)]
    modes.append(pass_on(modes[1], "x", AHEAD))
    last_image = pass_on(images[1], "y", AHEAD)

    place = jnp.stack([lax.axis_index(axis) for axis in ("core", "x", "y")])
    turns = (0, 1, -1, 2)
    keep, send = product(place, modes, images, turns)
    received = lax.ppermute(send, "core", SWAP)
    keep_last, send_last = product(place, modes, [last_image], turns)
    received_last = lax.ppermute(send_last, "core", SWAP)
    partial = kernel_call(
        join_kernel, jax.ShapeDtypeStruct((4, 4, 64, 128), F32), moved=1_500_000
    )(keep, received, keep_last, received_last)
    near = lax.all_to_all(partial, "zl", 0, 0, tiled=True)
    near = pl.pallas_call(
        near_kernel,
        out_shape=jax.ShapeDtypeStruct((4, 64, 128), F32),
        in_specs=[pl.BlockSpec(memory_space=pltpu.SMEM), whole],
        out_specs=whole,
        compiler_params=pltpu.CompilerParams(vmem_limit_bytes=VMEM_BYTES),
    )(place, near)
    far = lax.all_to_all(near, "zh", 0, 0, tiled=True)
    piece = kernel_call(
        functools.partial(far_kernel, weight), jax.ShapeDtypeStruct((64, 128), F32), moved=200_000
    )(far)
    reduced = turn_over(piece).T
    return reduced, advected.reshape(basis.shape), r_factor


def solution(mesh):
    fine = Mesh(mesh.devices.reshape(4, 4, 2, 4, 4), AXES)
    placed = (
        P(None, SPACE, None, None, MODE),
        P(None, SPACE, None, None),
        P(None, None, SPACE, None, None),
        P(SPACE, None, None),
    )
    return jax.shard_map(
        body,
        mesh=fine,
        in_specs=placed,
        out_specs=(P(MODE, SPACE), P(None, SPACE, None, None, MODE), P(MODE, None)),
        check_vma=False,
    )
```

```python
import functools

import jax
import jax.numpy as jnp
from jax import lax
from jax.experimental import pallas as pl
from jax.experimental.pallas import tpu as pltpu
from jax.sharding import Mesh
from jax.sharding import PartitionSpec as P

F32 = jnp.float32
BF16 = jnp.bfloat16
AXES = ("zh", "zl", "core", "y", "x")
SPACE = ("zh", "zl", "core")
MODE = ("y", "x")
VMEM_BYTES = 16 * 1024 * 1024


def kernel_call(body, outs, scratch=(), flops=0, moved=0, name=None):
    whole = pl.BlockSpec(memory_space=pltpu.VMEM)
    multiple = isinstance(outs, (tuple, list))
    return pl.pallas_call(
        body,
        out_shape=outs,
        out_specs=[whole] * len(outs) if multiple else whole,
        scratch_shapes=list(scratch),
        compiler_params=pltpu.CompilerParams(vmem_limit_bytes=VMEM_BYTES),
        cost_estimate=pl.CostEstimate(flops=flops, bytes_accessed=moved, transcendentals=0),
        name=name,
    )


def split3(a):
    high = a.astype(BF16)
    rest = a - high.astype(F32)
    mid = rest.astype(BF16)
    low = (rest - mid.astype(F32)).astype(BF16)
    return high, mid, low


def dot_rows(a, b):
    return lax.dot_general(a, b, (((0,), (0,)), ((), ())), preferred_element_type=F32)


def coefficient_kernel(place_ref, flow_ref, gradient_ref, viscosity_ref, out_ref):
    del place_ref

    def wide(values):
        return jnp.concatenate([values[x] for x in range(values.shape[0])], axis=1)

    nu = wide(viscosity_ref[...])
    level = lax.broadcasted_iota(jnp.int32, nu.shape, 0)
    for d in range(3):
        half = 0.5 * wide(flow_ref[d])
        ahead, back = nu - half, nu + half
        if d == 2:
            ahead = jnp.where(level < nu.shape[0] - 1, ahead, 0.0)
            back = jnp.where(level > 0, back, 0.0)
        out_ref[2 * d] = ahead
        out_ref[2 * d + 1] = back
    for i in range(3):
        for j in range(3):
            own = wide(gradient_ref[i, j])
            out_ref[6 + 3 * i + j] = own + 6.0 * nu if i == j else own


def gram_kernel(x_ref, out_ref):
    rows = x_ref.shape[0]
    step = rows // 3
    total = jnp.zeros((256, 256), F32)
    side = jnp.zeros((128, 128), F32)
    for start in range(0, rows, step):
        high, mid, low = split3(x_ref[start : start + step, :])
        both = jnp.concatenate([high, mid], axis=1)
        total = total + dot_rows(both, both)
        side = side + dot_rows(high, low)
    gram = total[:128, :128] + total[:128, 128:] + total[128:, :128] + total[128:, 128:]
    gram = gram + side + side.T
    top, bottom = gram[:64], gram[64:]
    row = lax.broadcasted_iota(jnp.int32, (64, 128), 0)
    lane = lax.broadcasted_iota(jnp.int32, (64, 128), 1)
    packed = jnp.where((lane >= 64) & (row >= lane - 64), pltpu.roll(top, 64, 1), bottom)
    diagonal = jnp.sum(jnp.where(row == lane - 64, bottom, 0.0), axis=0, keepdims=True)
    out_ref[:64, :] = packed
    out_ref[64:, :] = jnp.broadcast_to(diagonal, (8, 128))


def times_inverse(inverse):
    high, mid, low = (inverse[:, 128 * t : 128 * t + 128] for t in range(3))
    pair = jnp.concatenate([high, mid], axis=1)
    main = jnp.concatenate([pair, pair], axis=0)
    side = jnp.concatenate([low, high], axis=0)

    def times(values):
        h, m, l = split3(values)
        first = jnp.dot(jnp.concatenate([h, m], axis=1), main, preferred_element_type=F32)
        second = jnp.dot(jnp.concatenate([h, l], axis=1), side, preferred_element_type=F32)
        return first[:, :128] + (first[:, 128:] + second)

    return times


def modes_kernel(x_ref, inverse_ref, rounded_ref):
    times = times_inverse(inverse_ref[...])
    step = 1024
    for first in range(0, x_ref.shape[0], step):
        at = slice(first, first + step)
        rounded_ref[at, :] = times(x_ref[at, :]).astype(BF16)


def image_layer(x, x_ref, beside, coefficient_ref, out_ref, skipped=0):
    cells_x, cells_y, cells_z = x_ref.shape[1:4]
    values = [coefficient_ref[n] for n in range(15)]
    for y in range(cells_y):
        place = slice(x * cells_y + y, x * cells_y + y + 1)
        cell = [jnp.broadcast_to(v[:, place], (8, 128)) for v in values]
        east_c, west_c, north_c, south_c, upper_c, lower_c = cell[:6]
        center = [x_ref[i, x, y] for i in range(3)]
        for i in range(3):
            image = east_c * beside(i, x + 1, y) + west_c * beside(i, x - 1, y)
            if y + 1 < cells_y:
                image = image + north_c * x_ref[i, x, y + 1]
            if y > 0:
                image = image + south_c * x_ref[i, x, y - 1]
            image = image + upper_c * pltpu.roll(center[i], 7, 0)
            image = image + lower_c * pltpu.roll(center[i], 1, 0)
            for j in range(3):
                image = image - cell[6 + 3 * i + j] * center[j]
            layer = i * (cells_x - 2 * skipped) + x - skipped
            first = (layer * cells_y + y) * cells_z
            out_ref[first : first + cells_z, :] = image


def inner_kernel(x_ref, coefficient_ref, raw_ref):
    for x in range(1, x_ref.shape[1] - 1):
        image_layer(x, x_ref, lambda i, x, y: x_ref[i, x, y], coefficient_ref, raw_ref, 1)


def image_kernel(
    x_ref, west_ref, east_ref, coefficient_ref, inner_ref, inverse_ref,
    advected_ref, rounded_ref, work_ref, sems,
):
    cells_x, cells_y, cells_z = x_ref.shape[1:4]
    layer = cells_y * cells_z

    def beside(i, x, y):
        if x < 0:
            return west_ref[i, 0, y]
        return x_ref[i, x, y] if x < cells_x else east_ref[i, 0, y]

    times = times_inverse(inverse_ref[...])
    sent = []

    def finish(source_ref, x, layers, skipped=0):
        for i in range(3):
            at = pl.ds((i * cells_x + x) * layer, layers * layer)
            source = pl.ds((i * (cells_x - 2 * skipped) + x - skipped) * layer, layers * layer)
            advected = times(source_ref[source, :])
            work_ref[at, :] = advected
            rounded_ref[at, :] = advected.astype(BF16)
            sent.append(
                pltpu.make_async_copy(work_ref.at[at, :], advected_ref.at[at, :], sems.at[len(sent)])
            )
            sent[-1].start()

    half = cells_x // 2
    finish(inner_ref, 1, half - 1, 1)
    image_layer(0, x_ref, beside, coefficient_ref, work_ref)
    finish(inner_ref, half, half - 1, 1)
    image_layer(cells_x - 1, x_ref, beside, coefficient_ref, work_ref)
    finish(work_ref, 0, 1)
    finish(work_ref, cells_x - 1, 1)
    for copy in sent:
        copy.wait()


def pair_kernel(a_ref, b_ref, out_ref):
    total = a_ref[...] + b_ref[...]
    for n in range(4):
        out_ref[n] = total


def four_kernel(parts_ref, out_ref):
    total = (parts_ref[0] + parts_ref[1]) + (parts_ref[2] + parts_ref[3])
    for n in range(4):
        out_ref[n] = total


def factor_kernel(weight, parts_ref, west_ref, east_ref, inner_ref, r_ref, inverse_ref):
    del west_ref, east_ref, inner_ref
    packed = parts_ref[0] + parts_ref[1] + (parts_ref[2] + parts_ref[3])
    packed = packed * weight
    top = packed[:64]
    diagonal = packed[64:65]
    turned = pltpu.roll(top, 64, 1)
    across = jnp.concatenate([top, turned], axis=0).T
    row = lax.broadcasted_iota(jnp.int32, (64, 128), 0)
    lane = lax.broadcasted_iota(jnp.int32, (64, 128), 1)
    upper_half = jnp.where((lane < 64) & (row >= lane), turned, across[64:])
    lower_half = jnp.where(
        (lane < 64) | (row < lane - 64), top, jnp.where(row > lane - 64, across[:64], diagonal)
    )
    a = [upper_half[8 * b : 8 * b + 8] for b in range(8)]
    a += [lower_half[8 * b : 8 * b + 8] for b in range(8)]
    sub = lax.broadcasted_iota(jnp.int32, (8, 128), 0)
    col = lax.broadcasted_iota(jnp.int32, (8, 128), 1)
    w = [jnp.where(sub + 8 * b == col, 1.0, 0.0).astype(F32) for b in range(16)]

    def spread_row(values, t):
        return jnp.broadcast_to(values[t : t + 1, :], (8, 128))

    def combine(columns, values):
        terms = [c * spread_row(values, t) for t, c in enumerate(columns)]
        while len(terms) > 1:
            terms = [p + q for p, q in zip(terms[::2], terms[1::2])]
        return terms[0]

    inverse_rows = []
    for k in range(16):
        r, v = a[k], w[k]
        e = {}
        for j in range(8):
            column = jnp.broadcast_to(r[:, 8 * k + j : 8 * k + j + 1], (8, 128))
            for i in range(j + 1):
                e[i, j] = spread_row(column, i)
        inv = {}
        u = {}
        for t in range(8):
            scale = lax.rsqrt(e[t, t])
            inv[t, t] = scale
            for j in range(t + 1, 8):
                u[t, j] = e[t, j] * scale
            for i in range(t + 1, 8):
                for j in range(i, 8):
                    e[i, j] = e[i, j] - u[t, i] * u[t, j]
        for t in range(8):
            for i in range(t + 1, 8):
                total = u[t, i] * inv[t, t]
                for m in range(t + 1, i):
                    total = total + u[m, i] * inv[m, t]
                inv[i, t] = -inv[i, i] * total
        columns, turned_columns = [], []
        for j in range(8):
            column = jnp.zeros((8, 128), F32)
            for i in range(j, 8):
                column = jnp.where(sub == i, inv[i, j], column)
            columns.append(column)
            column = jnp.zeros((8, 128), F32)
            for i in range(j + 1):
                column = jnp.where(sub == i, inv[j, i], column)
            turned_columns.append(column)
        upper = combine(columns, r)
        lower_inverse = combine(columns, v)
        r_ref[8 * k : 8 * k + 8, :] = jnp.where(col >= sub + 8 * k, upper, 0.0)
        inverse_rows.append(lower_inverse)
        if k < 15:
            z = combine(turned_columns, upper)
            zv = combine(turned_columns, lower_inverse)
            z_rows = [spread_row(z, t) for t in range(8)]
            zv_rows = [spread_row(zv, t) for t in range(8)]
            for b in range(k + 1, 16):
                cs = [
                    jnp.broadcast_to(a[b][:, 8 * k + j : 8 * k + j + 1], (8, 128)) for j in range(8)
                ]
                s = [c * z_rows[j] for j, c in enumerate(cs)]
                sv = [c * zv_rows[j] for j, c in enumerate(cs)]
                a[b] = a[b] - (((s[0] + s[1]) + (s[2] + s[3])) + ((s[4] + s[5]) + (s[6] + s[7])))
                w[b] = w[b] - (
                    ((sv[0] + sv[1]) + (sv[2] + sv[3])) + ((sv[4] + sv[5]) + (sv[6] + sv[7]))
                )
    r_inverse = jnp.concatenate(inverse_rows, axis=0).T
    high, mid, low = split3(r_inverse)
    inverse_ref[:, :128] = high
    inverse_ref[:, 128:256] = mid
    inverse_ref[:, 256:] = low


def product_kernel(mode_turns, place_ref, *refs):
    mode_refs = refs[: len(mode_turns)]
    image_refs = refs[len(mode_turns) : -3]
    keep_ref, send_ref, total_ref = refs[-3:]
    half = mode_refs[0].shape[0] // 2
    for part in range(2):
        at = slice(part * half, part * half + half)
        wide = [
            jnp.concatenate([r[at, :] for r in group], axis=1) for group in (mode_refs, image_refs)
        ]
        product = dot_rows(wide[1], wide[0])
        if part == 0:
            total_ref[...] = product
        else:
            total_ref[...] += product
    core, x = place_ref[0], place_ref[1]
    ahead = 2 * core - 1
    for a, mode_turn in enumerate(mode_turns):
        panel_x = lax.rem(x + 4 + ahead * mode_turn, 4)
        lanes = slice(128 * a, 128 * a + 128)
        for b in range(len(image_refs)):
            slot = b if b == 0 else b + core * (3 - 2 * b)
            mine = pl.ds(pl.multiple_of(128 * b + 64 * core, 64), 64)
            other = pl.ds(pl.multiple_of(128 * b + 64 * (1 - core), 64), 64)
            keep_ref[panel_x, slot] = total_ref[mine, lanes]
            send_ref[panel_x, slot] = total_ref[other, lanes]


def product(place, modes, images, mode_turns):
    shape = jax.ShapeDtypeStruct((4, len(images), 64, 128), F32)
    whole = pl.BlockSpec(memory_space=pltpu.VMEM)
    return pl.pallas_call(
        functools.partial(product_kernel, mode_turns),
        out_shape=(shape, shape),
        in_specs=[pl.BlockSpec(memory_space=pltpu.SMEM)] + [whole] * (len(modes) + len(images)),
        out_specs=[whole, whole],
        scratch_shapes=[pltpu.VMEM((128 * len(images), 128 * len(modes)), F32)],
        compiler_params=pltpu.CompilerParams(vmem_limit_bytes=VMEM_BYTES),
        cost_estimate=pl.CostEstimate(
            flops=100_000_000 * len(modes) * len(images), bytes_accessed=6_000_000, transcendentals=0
        ),
    )(place, *modes, *images)


def join_kernel(keep_ref, received_ref, keep_last_ref, received_last_ref, out_ref):
    for n in range(4):
        out_ref[n, :3] = keep_ref[n] + received_ref[n]
        out_ref[n, 3] = keep_last_ref[n, 0] + received_last_ref[n, 0]


def near_kernel(place_ref, parts_ref, out_ref):
    y = place_ref[2]
    for slot, turn in enumerate((0, -1, 1, 2)):
        out_ref[lax.rem(y + 4 + turn, 4)] = (parts_ref[0, slot] + parts_ref[1, slot]) + (
            parts_ref[2, slot] + parts_ref[3, slot]
        )


def far_kernel(weight, parts_ref, out_ref):
    out_ref[...] = ((parts_ref[0] + parts_ref[1]) + (parts_ref[2] + parts_ref[3])) * weight


AHEAD = [(i, (i + 1) % 4) for i in range(4)] + [(4 + i, 4 + (i + 3) % 4) for i in range(4)]
BACK = [(target, source) for source, target in AHEAD]


def pass_on(block, axis, pairs):
    return lax.ppermute(block, ("core", axis), pairs)


SWAP = [(0, 1), (1, 0)]


def copies(block, count):
    return jnp.broadcast_to(block[None], (count,) + block.shape)


def turn_over(block):
    pairs = [(4 * zl + x, 4 * x + zl) for zl in range(4) for x in range(4)]
    return lax.ppermute(block, ("zl", "x"), pairs)


def body(basis, mean_flow, flow_gradient, viscosity):
    _, cells_x, cells_y, cells_z, width = basis.shape
    rows = 3 * cells_x * cells_y * cells_z
    blocks = 32
    weight = 1.0 / (rows * blocks)
    flat = basis.reshape(rows, width)
    west = lax.ppermute(basis[:, -1:], SPACE, [(i, i + 1) for i in range(blocks - 1)])
    east = lax.ppermute(basis[:, :1], SPACE, [(i + 1, i) for i in range(blocks - 1)])

    packed = jax.ShapeDtypeStruct((72, 128), F32)
    packed4 = jax.ShapeDtypeStruct((4, 72, 128), F32)
    gram = kernel_call(gram_kernel, packed, flops=600_000_000, moved=1_600_000)(flat)
    place = jnp.stack([lax.axis_index(axis) for axis in ("core", "x", "y")])
    whole = pl.BlockSpec(memory_space=pltpu.VMEM)
    scalars = pl.BlockSpec(memory_space=pltpu.SMEM)
    coefficients = pl.pallas_call(
        coefficient_kernel,
        out_shape=jax.ShapeDtypeStruct((15, cells_z, cells_x * cells_y), F32),
        in_specs=[scalars, whole, whole, whole],
        out_specs=whole,
        compiler_params=pltpu.CompilerParams(vmem_limit_bytes=VMEM_BYTES),
        cost_estimate=pl.CostEstimate(flops=200_000, bytes_accessed=500_000, transcendentals=0),
    )(place, mean_flow.swapaxes(2, 3), flow_gradient.swapaxes(3, 4), viscosity.swapaxes(1, 2))
    inner_rows = 3 * (cells_x - 2) * cells_y * cells_z
    inner = kernel_call(
        inner_kernel, jax.ShapeDtypeStruct((inner_rows, width), F32), flops=25_000_000, moved=3_000_000
    )(basis, coefficients)
    received = lax.ppermute(gram, "core", SWAP)
    mine = kernel_call(pair_kernel, packed4, moved=200_000)(gram, received)
    near = lax.all_to_all(mine, "zl", 0, 0, tiled=True)
    near = kernel_call(four_kernel, packed4, moved=300_000)(near)
    parts = lax.all_to_all(near, "zh", 0, 0, tiled=True)
    whole = pl.BlockSpec(memory_space=pltpu.VMEM)
    anywhere = pl.BlockSpec(memory_space=pl.ANY)
    r_factor, inverse = pl.pallas_call(
        functools.partial(factor_kernel, weight),
        out_shape=(
            jax.ShapeDtypeStruct((128, 128), F32),
            jax.ShapeDtypeStruct((128, 384), BF16),
        ),
        in_specs=[whole, anywhere, anywhere, anywhere],
        out_specs=[whole, whole],
        compiler_params=pltpu.CompilerParams(vmem_limit_bytes=VMEM_BYTES),
        cost_estimate=pl.CostEstimate(flops=10_000_000, bytes_accessed=400_000, transcendentals=0),
    )(parts, west, east, inner)
    rounded = pl.pallas_call(
        modes_kernel,
        out_shape=jax.ShapeDtypeStruct((rows, width), BF16),
        in_specs=[whole, whole],
        out_specs=whole,
        compiler_params=pltpu.CompilerParams(vmem_limit_bytes=VMEM_BYTES),
        cost_estimate=pl.CostEstimate(
            flops=600_000_000, bytes_accessed=2_400_000, transcendentals=0
        ),
    )(flat, inverse)
    modes = [rounded, pass_on(rounded, "x", AHEAD), pass_on(rounded, "x", BACK)]
    advected, rounded_image = pl.pallas_call(
        image_kernel,
        out_shape=(
            jax.ShapeDtypeStruct((rows, width), F32),
            jax.ShapeDtypeStruct((rows, width), BF16),
        ),
        in_specs=[whole] * 6,
        out_specs=[anywhere, whole],
        scratch_shapes=[
            pltpu.VMEM((rows, width), F32),
            pltpu.SemaphoreType.DMA((12,)),
        ],
        compiler_params=pltpu.CompilerParams(vmem_limit_bytes=VMEM_BYTES),
        cost_estimate=pl.CostEstimate(
            flops=600_000_000, bytes_accessed=5_000_000, transcendentals=0
        ),
    )(
        basis,
        west,
        east,
        coefficients,
        inner,
        inverse,
    )
    images = [rounded_image, pass_on(rounded_image, "y", AHEAD), pass_on(rounded_image, "y", BACK)]
    modes.append(pass_on(modes[1], "x", AHEAD))
    last_image = pass_on(images[1], "y", AHEAD)

    turns = (0, 1, -1, 2)
    keep, send = product(place, modes, images, turns)
    received = lax.ppermute(send, "core", SWAP)
    keep_last, send_last = product(place, modes, [last_image], turns)
    received_last = lax.ppermute(send_last, "core", SWAP)
    partial = kernel_call(
        join_kernel, jax.ShapeDtypeStruct((4, 4, 64, 128), F32), moved=1_500_000
    )(keep, received, keep_last, received_last)
    near = lax.all_to_all(partial, "zl", 0, 0, tiled=True)
    near = pl.pallas_call(
        near_kernel,
        out_shape=jax.ShapeDtypeStruct((4, 64, 128), F32),
        in_specs=[pl.BlockSpec(memory_space=pltpu.SMEM), whole],
        out_specs=whole,
        compiler_params=pltpu.CompilerParams(vmem_limit_bytes=VMEM_BYTES),
    )(place, near)
    far = lax.all_to_all(near, "zh", 0, 0, tiled=True)
    piece = kernel_call(
        functools.partial(far_kernel, weight), jax.ShapeDtypeStruct((64, 128), F32), moved=200_000
    )(far)
    reduced = turn_over(piece).T
    return reduced, advected.reshape(basis.shape), r_factor


def solution(mesh):
    fine = Mesh(mesh.devices.reshape(4, 4, 2, 4, 4), AXES)
    placed = (
        P(None, SPACE, None, None, MODE),
        P(None, SPACE, None, None),
        P(None, None, SPACE, None, None),
        P(SPACE, None, None),
    )
    return jax.shard_map(
        body,
        mesh=fine,
        in_specs=placed,
        out_specs=(P(MODE, SPACE), P(None, SPACE, None, None, MODE), P(MODE, None)),
        check_vma=False,
    )
```

```python
import functools

import jax
import jax.numpy as jnp
from jax import lax
from jax.experimental import pallas as pl
from jax.experimental.pallas import tpu as pltpu
from jax.sharding import Mesh
from jax.sharding import PartitionSpec as P

F32 = jnp.float32
BF16 = jnp.bfloat16
AXES = ("zh", "zl", "core", "y", "x")
SPACE = ("zh", "zl", "core")
MODE = ("y", "x")
VMEM_BYTES = 16 * 1024 * 1024


def kernel_call(body, outs, scratch=(), flops=0, moved=0, name=None):
    whole = pl.BlockSpec(memory_space=pltpu.VMEM)
    multiple = isinstance(outs, (tuple, list))
    return pl.pallas_call(
        body,
        out_shape=outs,
        out_specs=[whole] * len(outs) if multiple else whole,
        scratch_shapes=list(scratch),
        compiler_params=pltpu.CompilerParams(vmem_limit_bytes=VMEM_BYTES),
        cost_estimate=pl.CostEstimate(flops=flops, bytes_accessed=moved, transcendentals=0),
        name=name,
    )


def split3(a):
    high = a.astype(BF16)
    rest = a - high.astype(F32)
    mid = rest.astype(BF16)
    low = (rest - mid.astype(F32)).astype(BF16)
    return high, mid, low


def dot_rows(a, b):
    return lax.dot_general(a, b, (((0,), (0,)), ((), ())), preferred_element_type=F32)


def coefficient_kernel(place_ref, flow_ref, gradient_ref, viscosity_ref, out_ref):
    del place_ref

    def wide(values):
        return jnp.concatenate([values[x] for x in range(values.shape[0])], axis=1)

    nu = wide(viscosity_ref[...])
    level = lax.broadcasted_iota(jnp.int32, nu.shape, 0)
    for d in range(3):
        half = 0.5 * wide(flow_ref[d])
        ahead, back = nu - half, nu + half
        if d == 2:
            ahead = jnp.where(level < nu.shape[0] - 1, ahead, 0.0)
            back = jnp.where(level > 0, back, 0.0)
        out_ref[2 * d] = ahead
        out_ref[2 * d + 1] = back
    for i in range(3):
        for j in range(3):
            own = wide(gradient_ref[i, j])
            out_ref[6 + 3 * i + j] = own + 6.0 * nu if i == j else own


def gram_kernel(x_ref, out_ref):
    rows = x_ref.shape[0]
    step = rows // 3
    total = jnp.zeros((256, 256), F32)
    side = jnp.zeros((128, 128), F32)
    for start in range(0, rows, step):
        high, mid, low = split3(x_ref[start : start + step, :])
        both = jnp.concatenate([high, mid], axis=1)
        total = total + dot_rows(both, both)
        side = side + dot_rows(high, low)
    gram = total[:128, :128] + total[:128, 128:] + total[128:, :128] + total[128:, 128:]
    gram = gram + side + side.T
    top, bottom = gram[:64], gram[64:]
    row = lax.broadcasted_iota(jnp.int32, (64, 128), 0)
    lane = lax.broadcasted_iota(jnp.int32, (64, 128), 1)
    packed = jnp.where((lane >= 64) & (row >= lane - 64), pltpu.roll(top, 64, 1), bottom)
    diagonal = jnp.sum(jnp.where(row == lane - 64, bottom, 0.0), axis=0, keepdims=True)
    out_ref[:64, :] = packed
    out_ref[64:, :] = jnp.broadcast_to(diagonal, (8, 128))


def times_inverse(inverse):
    high, mid, low = (inverse[:, 128 * t : 128 * t + 128] for t in range(3))
    pair = jnp.concatenate([high, mid], axis=1)
    main = jnp.concatenate([pair, pair], axis=0)
    side = jnp.concatenate([low, high], axis=0)

    def times(values):
        h, m, l = split3(values)
        first = jnp.dot(jnp.concatenate([h, m], axis=1), main, preferred_element_type=F32)
        second = jnp.dot(jnp.concatenate([h, l], axis=1), side, preferred_element_type=F32)
        return first[:, :128] + (first[:, 128:] + second)

    return times


def modes_kernel(x_ref, inverse_ref, rounded_ref):
    times = times_inverse(inverse_ref[...])
    step = 1024
    for first in range(0, x_ref.shape[0], step):
        at = slice(first, first + step)
        rounded_ref[at, :] = times(x_ref[at, :]).astype(BF16)


def image_layer(x, x_ref, beside, coefficient_ref, out_ref, skipped=0):
    cells_x, cells_y, cells_z = x_ref.shape[1:4]
    values = [coefficient_ref[n] for n in range(15)]
    for y in range(cells_y):
        place = slice(x * cells_y + y, x * cells_y + y + 1)
        cell = [jnp.broadcast_to(v[:, place], (8, 128)) for v in values]
        east_c, west_c, north_c, south_c, upper_c, lower_c = cell[:6]
        center = [x_ref[i, x, y] for i in range(3)]
        for i in range(3):
            image = east_c * beside(i, x + 1, y) + west_c * beside(i, x - 1, y)
            if y + 1 < cells_y:
                image = image + north_c * x_ref[i, x, y + 1]
            if y > 0:
                image = image + south_c * x_ref[i, x, y - 1]
            image = image + upper_c * pltpu.roll(center[i], 7, 0)
            image = image + lower_c * pltpu.roll(center[i], 1, 0)
            for j in range(3):
                image = image - cell[6 + 3 * i + j] * center[j]
            layer = i * (cells_x - 2 * skipped) + x - skipped
            first = (layer * cells_y + y) * cells_z
            out_ref[first : first + cells_z, :] = image


def inner_kernel(x_ref, coefficient_ref, raw_ref):
    for x in range(1, x_ref.shape[1] - 1):
        image_layer(x, x_ref, lambda i, x, y: x_ref[i, x, y], coefficient_ref, raw_ref, 1)


def image_kernel(
    x_ref, west_ref, east_ref, coefficient_ref, inner_ref, inverse_ref,
    advected_ref, rounded_ref, work_ref, sems,
):
    cells_x, cells_y, cells_z = x_ref.shape[1:4]
    layer = cells_y * cells_z

    def beside(i, x, y):
        if x < 0:
            return west_ref[i, 0, y]
        return x_ref[i, x, y] if x < cells_x else east_ref[i, 0, y]

    times = times_inverse(inverse_ref[...])
    sent = []

    def finish(source_ref, x, layers, skipped=0):
        for i in range(3):
            at = pl.ds((i * cells_x + x) * layer, layers * layer)
            source = pl.ds((i * (cells_x - 2 * skipped) + x - skipped) * layer, layers * layer)
            advected = times(source_ref[source, :])
            work_ref[at, :] = advected
            rounded_ref[at, :] = advected.astype(BF16)
            sent.append(
                pltpu.make_async_copy(work_ref.at[at, :], advected_ref.at[at, :], sems.at[len(sent)])
            )
            sent[-1].start()

    half = cells_x // 2
    finish(inner_ref, 1, half - 1, 1)
    image_layer(0, x_ref, beside, coefficient_ref, work_ref)
    finish(inner_ref, half, half - 1, 1)
    image_layer(cells_x - 1, x_ref, beside, coefficient_ref, work_ref)
    finish(work_ref, 0, 1)
    finish(work_ref, cells_x - 1, 1)
    for copy in sent:
        copy.wait()


def pair_kernel(a_ref, b_ref, out_ref):
    total = a_ref[...] + b_ref[...]
    for n in range(4):
        out_ref[n] = total


def four_kernel(parts_ref, out_ref):
    total = (parts_ref[0] + parts_ref[1]) + (parts_ref[2] + parts_ref[3])
    for n in range(4):
        out_ref[n] = total


def factor_kernel(weight, parts_ref, west_ref, east_ref, inner_ref, r_ref, inverse_ref):
    del west_ref, east_ref, inner_ref
    packed = parts_ref[0] + parts_ref[1] + (parts_ref[2] + parts_ref[3])
    packed = packed * weight
    top = packed[:64]
    diagonal = packed[64:65]
    turned = pltpu.roll(top, 64, 1)
    across = jnp.concatenate([top, turned], axis=0).T
    row = lax.broadcasted_iota(jnp.int32, (64, 128), 0)
    lane = lax.broadcasted_iota(jnp.int32, (64, 128), 1)
    upper_half = jnp.where((lane < 64) & (row >= lane), turned, across[64:])
    lower_half = jnp.where(
        (lane < 64) | (row < lane - 64), top, jnp.where(row > lane - 64, across[:64], diagonal)
    )
    a = [upper_half[8 * b : 8 * b + 8] for b in range(8)]
    a += [lower_half[8 * b : 8 * b + 8] for b in range(8)]
    sub = lax.broadcasted_iota(jnp.int32, (8, 128), 0)
    col = lax.broadcasted_iota(jnp.int32, (8, 128), 1)
    w = [jnp.where(sub + 8 * b == col, 1.0, 0.0).astype(F32) for b in range(16)]

    def spread_row(values, t):
        return jnp.broadcast_to(values[t : t + 1, :], (8, 128))

    def combine(columns, values):
        terms = [c * spread_row(values, t) for t, c in enumerate(columns)]
        while len(terms) > 1:
            terms = [p + q for p, q in zip(terms[::2], terms[1::2])]
        return terms[0]

    inverse_rows = []
    for k in range(16):
        r, v = a[k], w[k]
        e = {}
        for j in range(8):
            column = jnp.broadcast_to(r[:, 8 * k + j : 8 * k + j + 1], (8, 128))
            for i in range(j + 1):
                e[i, j] = spread_row(column, i)
        inv = {}
        u = {}
        for t in range(8):
            scale = lax.rsqrt(e[t, t])
            inv[t, t] = scale
            for j in range(t + 1, 8):
                u[t, j] = e[t, j] * scale
            for i in range(t + 1, 8):
                for j in range(i, 8):
                    e[i, j] = e[i, j] - u[t, i] * u[t, j]
        for t in range(8):
            for i in range(t + 1, 8):
                total = u[t, i] * inv[t, t]
                for m in range(t + 1, i):
                    total = total + u[m, i] * inv[m, t]
                inv[i, t] = -inv[i, i] * total
        columns, turned_columns = [], []
        for j in range(8):
            column = jnp.zeros((8, 128), F32)
            for i in range(j, 8):
                column = jnp.where(sub == i, inv[i, j], column)
            columns.append(column)
            column = jnp.zeros((8, 128), F32)
            for i in range(j + 1):
                column = jnp.where(sub == i, inv[j, i], column)
            turned_columns.append(column)
        upper = combine(columns, r)
        lower_inverse = combine(columns, v)
        r_ref[8 * k : 8 * k + 8, :] = jnp.where(col >= sub + 8 * k, upper, 0.0)
        inverse_rows.append(lower_inverse)
        if k < 15:
            z = combine(turned_columns, upper)
            zv = combine(turned_columns, lower_inverse)
            z_rows = [spread_row(z, t) for t in range(8)]
            zv_rows = [spread_row(zv, t) for t in range(8)]
            for b in range(k + 1, 16):
                cs = [
                    jnp.broadcast_to(a[b][:, 8 * k + j : 8 * k + j + 1], (8, 128)) for j in range(8)
                ]
                s = [c * z_rows[j] for j, c in enumerate(cs)]
                sv = [c * zv_rows[j] for j, c in enumerate(cs)]
                a[b] = a[b] - (((s[0] + s[1]) + (s[2] + s[3])) + ((s[4] + s[5]) + (s[6] + s[7])))
                w[b] = w[b] - (
                    ((sv[0] + sv[1]) + (sv[2] + sv[3])) + ((sv[4] + sv[5]) + (sv[6] + sv[7]))
                )
    r_inverse = jnp.concatenate(inverse_rows, axis=0).T
    high, mid, low = split3(r_inverse)
    inverse_ref[:, :128] = high
    inverse_ref[:, 128:256] = mid
    inverse_ref[:, 256:] = low


def product_kernel(mode_turns, place_ref, *refs):
    mode_refs = refs[: len(mode_turns)]
    image_refs = refs[len(mode_turns) : -3]
    keep_ref, send_ref, total_ref = refs[-3:]
    half = mode_refs[0].shape[0] // 2
    for part in range(2):
        at = slice(part * half, part * half + half)
        wide = [
            jnp.concatenate([r[at, :] for r in group], axis=1) for group in (mode_refs, image_refs)
        ]
        product = dot_rows(wide[1], wide[0])
        if part == 0:
            total_ref[...] = product
        else:
            total_ref[...] += product
    core, x, zl = place_ref[0], place_ref[1], place_ref[3]
    ahead = 2 * core - 1
    for a, mode_turn in enumerate(mode_turns):
        panel_x = lax.rem(x + 4 + ahead * mode_turn, 4)
        distance = lax.rem(panel_x + 4 - zl, 4)
        lanes = slice(128 * a, 128 * a + 128)
        for b in range(len(image_refs)):
            slot = b if b == 0 else b + core * (3 - 2 * b)
            mine = pl.ds(pl.multiple_of(128 * b + 64 * core, 64), 64)
            other = pl.ds(pl.multiple_of(128 * b + 64 * (1 - core), 64), 64)
            keep_ref[distance, slot] = total_ref[mine, lanes]
            send_ref[distance, slot] = total_ref[other, lanes]


def product(place, modes, images, mode_turns):
    shape = jax.ShapeDtypeStruct((4, len(images), 64, 128), F32)
    whole = pl.BlockSpec(memory_space=pltpu.VMEM)
    return pl.pallas_call(
        functools.partial(product_kernel, mode_turns),
        out_shape=(shape, shape),
        in_specs=[pl.BlockSpec(memory_space=pltpu.SMEM)] + [whole] * (len(modes) + len(images)),
        out_specs=[whole, whole],
        scratch_shapes=[pltpu.VMEM((128 * len(images), 128 * len(modes)), F32)],
        compiler_params=pltpu.CompilerParams(vmem_limit_bytes=VMEM_BYTES),
        cost_estimate=pl.CostEstimate(
            flops=100_000_000 * len(modes) * len(images), bytes_accessed=6_000_000, transcendentals=0
        ),
    )(place, *modes, *images)


def join_kernel(keep_ref, received_ref, keep_last_ref, received_last_ref, *out_refs):
    for n, out_ref in enumerate(out_refs):
        out_ref[:3] = keep_ref[n] + received_ref[n]
        out_ref[3] = keep_last_ref[n, 0] + received_last_ref[n, 0]


def near_kernel(place_ref, a_ref, b_ref, c_ref, d_ref, out_ref):
    y = place_ref[2]
    for slot, turn in enumerate((0, -1, 1, 2)):
        out_ref[lax.rem(y + 4 + turn, 4)] = (a_ref[slot] + b_ref[slot]) + (
            c_ref[slot] + d_ref[slot]
        )


def far_kernel(weight, parts_ref, out_ref):
    out_ref[...] = ((parts_ref[0] + parts_ref[1]) + (parts_ref[2] + parts_ref[3])) * weight


AHEAD = [(i, (i + 1) % 4) for i in range(4)] + [(4 + i, 4 + (i + 3) % 4) for i in range(4)]
BACK = [(target, source) for source, target in AHEAD]


def pass_on(block, axis, pairs):
    return lax.ppermute(block, ("core", axis), pairs)


SWAP = [(0, 1), (1, 0)]


def copies(block, count):
    return jnp.broadcast_to(block[None], (count,) + block.shape)


def turn_over(block):
    pairs = [(4 * zl + x, 4 * x + zl) for zl in range(4) for x in range(4)]
    return lax.ppermute(block, ("zl", "x"), pairs)


def body(basis, mean_flow, flow_gradient, viscosity):
    _, cells_x, cells_y, cells_z, width = basis.shape
    rows = 3 * cells_x * cells_y * cells_z
    blocks = 32
    weight = 1.0 / (rows * blocks)
    flat = basis.reshape(rows, width)
    west = lax.ppermute(basis[:, -1:], SPACE, [(i, i + 1) for i in range(blocks - 1)])
    east = lax.ppermute(basis[:, :1], SPACE, [(i + 1, i) for i in range(blocks - 1)])

    packed = jax.ShapeDtypeStruct((72, 128), F32)
    packed4 = jax.ShapeDtypeStruct((4, 72, 128), F32)
    gram = kernel_call(gram_kernel, packed, flops=600_000_000, moved=1_600_000)(flat)
    place = jnp.stack([lax.axis_index(axis) for axis in ("core", "x", "y", "zl")])
    whole = pl.BlockSpec(memory_space=pltpu.VMEM)
    scalars = pl.BlockSpec(memory_space=pltpu.SMEM)
    coefficients = pl.pallas_call(
        coefficient_kernel,
        out_shape=jax.ShapeDtypeStruct((15, cells_z, cells_x * cells_y), F32),
        in_specs=[scalars, whole, whole, whole],
        out_specs=whole,
        compiler_params=pltpu.CompilerParams(vmem_limit_bytes=VMEM_BYTES),
        cost_estimate=pl.CostEstimate(flops=200_000, bytes_accessed=500_000, transcendentals=0),
    )(place, mean_flow.swapaxes(2, 3), flow_gradient.swapaxes(3, 4), viscosity.swapaxes(1, 2))
    inner_rows = 3 * (cells_x - 2) * cells_y * cells_z
    inner = kernel_call(
        inner_kernel, jax.ShapeDtypeStruct((inner_rows, width), F32), flops=25_000_000, moved=3_000_000
    )(basis, coefficients)
    received = lax.ppermute(gram, "core", SWAP)
    mine = kernel_call(pair_kernel, packed4, moved=200_000)(gram, received)
    near = lax.all_to_all(mine, "zl", 0, 0, tiled=True)
    near = kernel_call(four_kernel, packed4, moved=300_000)(near)
    parts = lax.all_to_all(near, "zh", 0, 0, tiled=True)
    whole = pl.BlockSpec(memory_space=pltpu.VMEM)
    anywhere = pl.BlockSpec(memory_space=pl.ANY)
    r_factor, inverse = pl.pallas_call(
        functools.partial(factor_kernel, weight),
        out_shape=(
            jax.ShapeDtypeStruct((128, 128), F32),
            jax.ShapeDtypeStruct((128, 384), BF16),
        ),
        in_specs=[whole, anywhere, anywhere, anywhere],
        out_specs=[whole, whole],
        compiler_params=pltpu.CompilerParams(vmem_limit_bytes=VMEM_BYTES),
        cost_estimate=pl.CostEstimate(flops=10_000_000, bytes_accessed=400_000, transcendentals=0),
    )(parts, west, east, inner)
    rounded = pl.pallas_call(
        modes_kernel,
        out_shape=jax.ShapeDtypeStruct((rows, width), BF16),
        in_specs=[whole, whole],
        out_specs=whole,
        compiler_params=pltpu.CompilerParams(vmem_limit_bytes=VMEM_BYTES),
        cost_estimate=pl.CostEstimate(
            flops=600_000_000, bytes_accessed=2_400_000, transcendentals=0
        ),
    )(flat, inverse)
    modes = [rounded, pass_on(rounded, "x", AHEAD), pass_on(rounded, "x", BACK)]
    advected, rounded_image = pl.pallas_call(
        image_kernel,
        out_shape=(
            jax.ShapeDtypeStruct((rows, width), F32),
            jax.ShapeDtypeStruct((rows, width), BF16),
        ),
        in_specs=[whole] * 6,
        out_specs=[anywhere, whole],
        scratch_shapes=[
            pltpu.VMEM((rows, width), F32),
            pltpu.SemaphoreType.DMA((12,)),
        ],
        compiler_params=pltpu.CompilerParams(vmem_limit_bytes=VMEM_BYTES),
        cost_estimate=pl.CostEstimate(
            flops=600_000_000, bytes_accessed=5_000_000, transcendentals=0
        ),
    )(
        basis,
        west,
        east,
        coefficients,
        inner,
        inverse,
    )
    images = [rounded_image, pass_on(rounded_image, "y", AHEAD), pass_on(rounded_image, "y", BACK)]
    modes.append(pass_on(modes[1], "x", AHEAD))
    last_image = pass_on(images[1], "y", AHEAD)

    turns = (0, 1, -1, 2)
    keep, send = product(place, modes, images, turns)
    received = lax.ppermute(send, "core", SWAP)
    keep_last, send_last = product(place, modes, [last_image], turns)
    received_last = lax.ppermute(send_last, "core", SWAP)
    own, *others = kernel_call(
        join_kernel, [jax.ShapeDtypeStruct((4, 64, 128), F32)] * 4, moved=1_500_000
    )(keep, received, keep_last, received_last)
    arrived = [
        lax.ppermute(block, "zl", [(i, (i + n + 1) % 4) for i in range(4)])
        for n, block in enumerate(others)
    ]
    near = pl.pallas_call(
        near_kernel,
        out_shape=jax.ShapeDtypeStruct((4, 64, 128), F32),
        in_specs=[scalars] + [whole] * 4,
        out_specs=whole,
        compiler_params=pltpu.CompilerParams(vmem_limit_bytes=VMEM_BYTES),
    )(place, own, *arrived)
    far = lax.all_to_all(near, "zh", 0, 0, tiled=True)
    piece = kernel_call(
        functools.partial(far_kernel, weight), jax.ShapeDtypeStruct((64, 128), F32), moved=200_000
    )(far)
    reduced = turn_over(piece).T
    return reduced, advected.reshape(basis.shape), r_factor


def solution(mesh):
    fine = Mesh(mesh.devices.reshape(4, 4, 2, 4, 4), AXES)
    placed = (
        P(None, SPACE, None, None, MODE),
        P(None, SPACE, None, None),
        P(None, None, SPACE, None, None),
        P(SPACE, None, None),
    )
    return jax.shard_map(
        body,
        mesh=fine,
        in_specs=placed,
        out_specs=(P(MODE, SPACE), P(None, SPACE, None, None, MODE), P(MODE, None)),
        check_vma=False,
    )
```

```python
import functools

import jax
import jax.numpy as jnp
from jax import lax
from jax.experimental import pallas as pl
from jax.experimental.pallas import tpu as pltpu
from jax.sharding import Mesh
from jax.sharding import PartitionSpec as P

F32 = jnp.float32
BF16 = jnp.bfloat16
AXES = ("zh", "zl", "core", "y", "x")
SPACE = ("zh", "zl", "core")
MODE = ("y", "x")
VMEM_BYTES = 16 * 1024 * 1024


def kernel_call(body, outs, scratch=(), flops=0, moved=0, name=None):
    whole = pl.BlockSpec(memory_space=pltpu.VMEM)
    multiple = isinstance(outs, (tuple, list))
    return pl.pallas_call(
        body,
        out_shape=outs,
        out_specs=[whole] * len(outs) if multiple else whole,
        scratch_shapes=list(scratch),
        compiler_params=pltpu.CompilerParams(vmem_limit_bytes=VMEM_BYTES),
        cost_estimate=pl.CostEstimate(flops=flops, bytes_accessed=moved, transcendentals=0),
        name=name,
    )


def split3(a):
    high = a.astype(BF16)
    rest = a - high.astype(F32)
    mid = rest.astype(BF16)
    low = (rest - mid.astype(F32)).astype(BF16)
    return high, mid, low


def dot_rows(a, b):
    return lax.dot_general(a, b, (((0,), (0,)), ((), ())), preferred_element_type=F32)


def coefficient_kernel(place_ref, flow_ref, gradient_ref, viscosity_ref, out_ref):
    del place_ref

    def wide(values):
        return jnp.concatenate([values[x] for x in range(values.shape[0])], axis=1)

    nu = wide(viscosity_ref[...])
    level = lax.broadcasted_iota(jnp.int32, nu.shape, 0)
    for d in range(3):
        half = 0.5 * wide(flow_ref[d])
        ahead, back = nu - half, nu + half
        if d == 2:
            ahead = jnp.where(level < nu.shape[0] - 1, ahead, 0.0)
            back = jnp.where(level > 0, back, 0.0)
        out_ref[2 * d] = ahead
        out_ref[2 * d + 1] = back
    for i in range(3):
        for j in range(3):
            own = wide(gradient_ref[i, j])
            out_ref[6 + 3 * i + j] = own + 6.0 * nu if i == j else own


def gram_kernel(x_ref, out_ref):
    rows = x_ref.shape[0]
    step = rows // 3
    total = jnp.zeros((256, 256), F32)
    side = jnp.zeros((128, 128), F32)
    for start in range(0, rows, step):
        high, mid, low = split3(x_ref[start : start + step, :])
        both = jnp.concatenate([high, mid], axis=1)
        total = total + dot_rows(both, both)
        side = side + dot_rows(high, low)
    gram = total[:128, :128] + total[:128, 128:] + total[128:, :128] + total[128:, 128:]
    gram = gram + side + side.T
    top, bottom = gram[:64], gram[64:]
    row = lax.broadcasted_iota(jnp.int32, (64, 128), 0)
    lane = lax.broadcasted_iota(jnp.int32, (64, 128), 1)
    packed = jnp.where((lane >= 64) & (row >= lane - 64), pltpu.roll(top, 64, 1), bottom)
    diagonal = jnp.sum(jnp.where(row == lane - 64, bottom, 0.0), axis=0, keepdims=True)
    out_ref[:64, :] = packed
    out_ref[64:, :] = jnp.broadcast_to(diagonal, (8, 128))


def times_inverse(inverse):
    high, mid, low = (inverse[:, 128 * t : 128 * t + 128] for t in range(3))
    pair = jnp.concatenate([high, mid], axis=1)
    main = jnp.concatenate([pair, pair], axis=0)
    side = jnp.concatenate([low, high], axis=0)

    def times(values):
        h, m, l = split3(values)
        first = jnp.dot(jnp.concatenate([h, m], axis=1), main, preferred_element_type=F32)
        second = jnp.dot(jnp.concatenate([h, l], axis=1), side, preferred_element_type=F32)
        return first[:, :128] + (first[:, 128:] + second)

    return times


def modes_kernel(x_ref, inverse_ref, rounded_ref):
    times = times_inverse(inverse_ref[...])
    step = 1024
    for first in range(0, x_ref.shape[0], step):
        at = slice(first, first + step)
        rounded_ref[at, :] = times(x_ref[at, :]).astype(BF16)


def image_layer(x, x_ref, beside, coefficient_ref, out_ref, skipped=0):
    cells_x, cells_y, cells_z = x_ref.shape[1:4]
    values = [coefficient_ref[n] for n in range(15)]
    for y in range(cells_y):
        place = slice(x * cells_y + y, x * cells_y + y + 1)
        cell = [jnp.broadcast_to(v[:, place], (8, 128)) for v in values]
        east_c, west_c, north_c, south_c, upper_c, lower_c = cell[:6]
        center = [x_ref[i, x, y] for i in range(3)]
        for i in range(3):
            image = east_c * beside(i, x + 1, y) + west_c * beside(i, x - 1, y)
            if y + 1 < cells_y:
                image = image + north_c * x_ref[i, x, y + 1]
            if y > 0:
                image = image + south_c * x_ref[i, x, y - 1]
            image = image + upper_c * pltpu.roll(center[i], 7, 0)
            image = image + lower_c * pltpu.roll(center[i], 1, 0)
            for j in range(3):
                image = image - cell[6 + 3 * i + j] * center[j]
            layer = i * (cells_x - 2 * skipped) + x - skipped
            first = (layer * cells_y + y) * cells_z
            out_ref[first : first + cells_z, :] = image


def inner_kernel(x_ref, coefficient_ref, raw_ref):
    for x in range(1, x_ref.shape[1] - 1):
        image_layer(x, x_ref, lambda i, x, y: x_ref[i, x, y], coefficient_ref, raw_ref, 1)


def image_kernel(
    x_ref, west_ref, east_ref, coefficient_ref, inner_ref, inverse_ref,
    advected_ref, rounded_ref, work_ref, sems,
):
    cells_x, cells_y, cells_z = x_ref.shape[1:4]
    layer = cells_y * cells_z

    def beside(i, x, y):
        if x < 0:
            return west_ref[i, 0, y]
        return x_ref[i, x, y] if x < cells_x else east_ref[i, 0, y]

    times = times_inverse(inverse_ref[...])
    sent = []

    def finish(source_ref, x, layers, skipped=0):
        for i in range(3):
            at = pl.ds((i * cells_x + x) * layer, layers * layer)
            source = pl.ds((i * (cells_x - 2 * skipped) + x - skipped) * layer, layers * layer)
            advected = times(source_ref[source, :])
            work_ref[at, :] = advected
            rounded_ref[at, :] = advected.astype(BF16)
            sent.append(
                pltpu.make_async_copy(work_ref.at[at, :], advected_ref.at[at, :], sems.at[len(sent)])
            )
            sent[-1].start()

    half = cells_x // 2
    finish(inner_ref, 1, half - 1, 1)
    image_layer(0, x_ref, beside, coefficient_ref, work_ref)
    finish(inner_ref, half, half - 1, 1)
    image_layer(cells_x - 1, x_ref, beside, coefficient_ref, work_ref)
    finish(work_ref, 0, 1)
    finish(work_ref, cells_x - 1, 1)
    for copy in sent:
        copy.wait()


def pair_kernel(a_ref, b_ref, out_ref):
    total = a_ref[...] + b_ref[...]
    for n in range(4):
        out_ref[n] = total


def four_kernel(parts_ref, out_ref):
    total = (parts_ref[0] + parts_ref[1]) + (parts_ref[2] + parts_ref[3])
    for n in range(4):
        out_ref[n] = total


def factor_kernel(weight, parts_ref, west_ref, east_ref, inner_ref, r_ref, inverse_ref):
    del west_ref, east_ref, inner_ref
    packed = parts_ref[0] + parts_ref[1] + (parts_ref[2] + parts_ref[3])
    packed = packed * weight
    top = packed[:64]
    diagonal = packed[64:65]
    turned = pltpu.roll(top, 64, 1)
    across = jnp.concatenate([top, turned], axis=0).T
    row = lax.broadcasted_iota(jnp.int32, (64, 128), 0)
    lane = lax.broadcasted_iota(jnp.int32, (64, 128), 1)
    upper_half = jnp.where((lane < 64) & (row >= lane), turned, across[64:])
    lower_half = jnp.where(
        (lane < 64) | (row < lane - 64), top, jnp.where(row > lane - 64, across[:64], diagonal)
    )
    a = [upper_half[8 * b : 8 * b + 8] for b in range(8)]
    a += [lower_half[8 * b : 8 * b + 8] for b in range(8)]
    sub = lax.broadcasted_iota(jnp.int32, (8, 128), 0)
    col = lax.broadcasted_iota(jnp.int32, (8, 128), 1)
    w = [jnp.where(sub + 8 * b == col, 1.0, 0.0).astype(F32) for b in range(16)]

    def spread_row(values, t):
        return jnp.broadcast_to(values[t : t + 1, :], (8, 128))

    def combine(columns, values):
        terms = [c * spread_row(values, t) for t, c in enumerate(columns)]
        while len(terms) > 1:
            terms = [p + q for p, q in zip(terms[::2], terms[1::2])]
        return terms[0]

    inverse_rows = []
    for k in range(16):
        r, v = a[k], w[k]
        e = {}
        for j in range(8):
            column = jnp.broadcast_to(r[:, 8 * k + j : 8 * k + j + 1], (8, 128))
            for i in range(j + 1):
                e[i, j] = spread_row(column, i)
        inv = {}
        u = {}
        for t in range(8):
            scale = lax.rsqrt(e[t, t])
            inv[t, t] = scale
            for j in range(t + 1, 8):
                u[t, j] = e[t, j] * scale
            for i in range(t + 1, 8):
                for j in range(i, 8):
                    e[i, j] = e[i, j] - u[t, i] * u[t, j]
        for t in range(8):
            for i in range(t + 1, 8):
                total = u[t, i] * inv[t, t]
                for m in range(t + 1, i):
                    total = total + u[m, i] * inv[m, t]
                inv[i, t] = -inv[i, i] * total
        columns, turned_columns = [], []
        for j in range(8):
            column = jnp.zeros((8, 128), F32)
            for i in range(j, 8):
                column = jnp.where(sub == i, inv[i, j], column)
            columns.append(column)
            column = jnp.zeros((8, 128), F32)
            for i in range(j + 1):
                column = jnp.where(sub == i, inv[j, i], column)
            turned_columns.append(column)
        upper = combine(columns, r)
        lower_inverse = combine(columns, v)
        r_ref[8 * k : 8 * k + 8, :] = jnp.where(col >= sub + 8 * k, upper, 0.0)
        inverse_rows.append(lower_inverse)
        if k < 15:
            z = combine(turned_columns, upper)
            zv = combine(turned_columns, lower_inverse)
            z_rows = [spread_row(z, t) for t in range(8)]
            zv_rows = [spread_row(zv, t) for t in range(8)]
            for b in range(k + 1, 16):
                cs = [
                    jnp.broadcast_to(a[b][:, 8 * k + j : 8 * k + j + 1], (8, 128)) for j in range(8)
                ]
                s = [c * z_rows[j] for j, c in enumerate(cs)]
                sv = [c * zv_rows[j] for j, c in enumerate(cs)]
                a[b] = a[b] - (((s[0] + s[1]) + (s[2] + s[3])) + ((s[4] + s[5]) + (s[6] + s[7])))
                w[b] = w[b] - (
                    ((sv[0] + sv[1]) + (sv[2] + sv[3])) + ((sv[4] + sv[5]) + (sv[6] + sv[7]))
                )
    r_inverse = jnp.concatenate(inverse_rows, axis=0).T
    high, mid, low = split3(r_inverse)
    inverse_ref[:, :128] = high
    inverse_ref[:, 128:256] = mid
    inverse_ref[:, 256:] = low


def product_kernel(mode_turns, place_ref, *refs):
    mode_refs = refs[: len(mode_turns)]
    image_refs = refs[len(mode_turns) : -3]
    keep_ref, send_ref, total_ref = refs[-3:]
    half = mode_refs[0].shape[0] // 2
    for part in range(2):
        at = slice(part * half, part * half + half)
        wide = [
            jnp.concatenate([r[at, :] for r in group], axis=1) for group in (mode_refs, image_refs)
        ]
        product = dot_rows(wide[1], wide[0])
        if part == 0:
            total_ref[...] = product
        else:
            total_ref[...] += product
    core, x, zl = place_ref[0], place_ref[1], place_ref[3]
    ahead = 2 * core - 1
    for a, mode_turn in enumerate(mode_turns):
        panel_x = lax.rem(x + 4 + ahead * mode_turn, 4)
        distance = lax.rem(panel_x + 4 - zl, 4)
        lanes = slice(128 * a, 128 * a + 128)
        for b in range(len(image_refs)):
            slot = b if b == 0 else b + core * (3 - 2 * b)
            mine = pl.ds(pl.multiple_of(128 * b + 64 * core, 64), 64)
            other = pl.ds(pl.multiple_of(128 * b + 64 * (1 - core), 64), 64)
            keep_ref[distance, slot] = total_ref[mine, lanes]
            send_ref[distance, slot] = total_ref[other, lanes]


def product(place, modes, images, mode_turns):
    shape = jax.ShapeDtypeStruct((4, len(images), 64, 128), F32)
    whole = pl.BlockSpec(memory_space=pltpu.VMEM)
    return pl.pallas_call(
        functools.partial(product_kernel, mode_turns),
        out_shape=(shape, shape),
        in_specs=[pl.BlockSpec(memory_space=pltpu.SMEM)] + [whole] * (len(modes) + len(images)),
        out_specs=[whole, whole],
        scratch_shapes=[pltpu.VMEM((128 * len(images), 128 * len(modes)), F32)],
        compiler_params=pltpu.CompilerParams(vmem_limit_bytes=VMEM_BYTES),
        cost_estimate=pl.CostEstimate(
            flops=100_000_000 * len(modes) * len(images), bytes_accessed=6_000_000, transcendentals=0
        ),
    )(place, *modes, *images)


def ahead_kernel(keep_ref, received_ref, last_ref, out_ref):
    del last_ref
    out_ref[...] = keep_ref[2] + received_ref[2]


def next_kernel(keep_ref, received_ref, keep_last_ref, received_last_ref, ahead_ref, next_ref):
    del ahead_ref
    next_ref[:3] = keep_ref[1] + received_ref[1]
    next_ref[3] = keep_last_ref[1, 0] + received_last_ref[1, 0]


def rest_kernel(
    keep_ref, received_ref, keep_last_ref, received_last_ref, arrived_ref,
    own_ref, back_ref, two_ref,
):
    del arrived_ref
    for n, out_ref in ((0, own_ref), (3, back_ref)):
        out_ref[:3] = keep_ref[n] + received_ref[n]
        out_ref[3] = keep_last_ref[n, 0] + received_last_ref[n, 0]
    two_ref[...] = keep_last_ref[2] + received_last_ref[2]


def near_kernel(place_ref, own_ref, next_ref, back_ref, first_ref, last_ref, out_ref):
    y = place_ref[2]
    for slot, turn in enumerate((0, -1, 1, 2)):
        two = first_ref[slot] if slot < 3 else last_ref[0]
        out_ref[lax.rem(y + 4 + turn, 4)] = (own_ref[slot] + next_ref[slot]) + (
            back_ref[slot] + two
        )


def near_move(block, distance):
    return lax.ppermute(block, "zl", [(i, (i + distance) % 4) for i in range(4)])


def far_kernel(weight, parts_ref, out_ref):
    out_ref[...] = ((parts_ref[0] + parts_ref[1]) + (parts_ref[2] + parts_ref[3])) * weight


AHEAD = [(i, (i + 1) % 4) for i in range(4)] + [(4 + i, 4 + (i + 3) % 4) for i in range(4)]
BACK = [(target, source) for source, target in AHEAD]


def pass_on(block, axis, pairs):
    return lax.ppermute(block, ("core", axis), pairs)


SWAP = [(0, 1), (1, 0)]


def copies(block, count):
    return jnp.broadcast_to(block[None], (count,) + block.shape)


def turn_over(block):
    pairs = [(4 * zl + x, 4 * x + zl) for zl in range(4) for x in range(4)]
    return lax.ppermute(block, ("zl", "x"), pairs)


def body(basis, mean_flow, flow_gradient, viscosity):
    _, cells_x, cells_y, cells_z, width = basis.shape
    rows = 3 * cells_x * cells_y * cells_z
    blocks = 32
    weight = 1.0 / (rows * blocks)
    flat = basis.reshape(rows, width)
    west = lax.ppermute(basis[:, -1:], SPACE, [(i, i + 1) for i in range(blocks - 1)])
    east = lax.ppermute(basis[:, :1], SPACE, [(i + 1, i) for i in range(blocks - 1)])

    packed = jax.ShapeDtypeStruct((72, 128), F32)
    packed4 = jax.ShapeDtypeStruct((4, 72, 128), F32)
    gram = kernel_call(gram_kernel, packed, flops=600_000_000, moved=1_600_000)(flat)
    place = jnp.stack([lax.axis_index(axis) for axis in ("core", "x", "y", "zl")])
    whole = pl.BlockSpec(memory_space=pltpu.VMEM)
    scalars = pl.BlockSpec(memory_space=pltpu.SMEM)
    coefficients = pl.pallas_call(
        coefficient_kernel,
        out_shape=jax.ShapeDtypeStruct((15, cells_z, cells_x * cells_y), F32),
        in_specs=[scalars, whole, whole, whole],
        out_specs=whole,
        compiler_params=pltpu.CompilerParams(vmem_limit_bytes=VMEM_BYTES),
        cost_estimate=pl.CostEstimate(flops=200_000, bytes_accessed=500_000, transcendentals=0),
    )(place, mean_flow.swapaxes(2, 3), flow_gradient.swapaxes(3, 4), viscosity.swapaxes(1, 2))
    inner_rows = 3 * (cells_x - 2) * cells_y * cells_z
    inner = kernel_call(
        inner_kernel, jax.ShapeDtypeStruct((inner_rows, width), F32), flops=25_000_000, moved=3_000_000
    )(basis, coefficients)
    received = lax.ppermute(gram, "core", SWAP)
    mine = kernel_call(pair_kernel, packed4, moved=200_000)(gram, received)
    near = lax.all_to_all(mine, "zl", 0, 0, tiled=True)
    near = kernel_call(four_kernel, packed4, moved=300_000)(near)
    parts = lax.all_to_all(near, "zh", 0, 0, tiled=True)
    whole = pl.BlockSpec(memory_space=pltpu.VMEM)
    anywhere = pl.BlockSpec(memory_space=pl.ANY)
    r_factor, inverse = pl.pallas_call(
        functools.partial(factor_kernel, weight),
        out_shape=(
            jax.ShapeDtypeStruct((128, 128), F32),
            jax.ShapeDtypeStruct((128, 384), BF16),
        ),
        in_specs=[whole, anywhere, anywhere, anywhere],
        out_specs=[whole, whole],
        compiler_params=pltpu.CompilerParams(vmem_limit_bytes=VMEM_BYTES),
        cost_estimate=pl.CostEstimate(flops=10_000_000, bytes_accessed=400_000, transcendentals=0),
    )(parts, west, east, inner)
    rounded = pl.pallas_call(
        modes_kernel,
        out_shape=jax.ShapeDtypeStruct((rows, width), BF16),
        in_specs=[whole, whole],
        out_specs=whole,
        compiler_params=pltpu.CompilerParams(vmem_limit_bytes=VMEM_BYTES),
        cost_estimate=pl.CostEstimate(
            flops=600_000_000, bytes_accessed=2_400_000, transcendentals=0
        ),
    )(flat, inverse)
    modes = [rounded, pass_on(rounded, "x", AHEAD), pass_on(rounded, "x", BACK)]
    advected, rounded_image = pl.pallas_call(
        image_kernel,
        out_shape=(
            jax.ShapeDtypeStruct((rows, width), F32),
            jax.ShapeDtypeStruct((rows, width), BF16),
        ),
        in_specs=[whole] * 6,
        out_specs=[anywhere, whole],
        scratch_shapes=[
            pltpu.VMEM((rows, width), F32),
            pltpu.SemaphoreType.DMA((12,)),
        ],
        compiler_params=pltpu.CompilerParams(vmem_limit_bytes=VMEM_BYTES),
        cost_estimate=pl.CostEstimate(
            flops=600_000_000, bytes_accessed=5_000_000, transcendentals=0
        ),
    )(
        basis,
        west,
        east,
        coefficients,
        inner,
        inverse,
    )
    images = [rounded_image, pass_on(rounded_image, "y", AHEAD), pass_on(rounded_image, "y", BACK)]
    modes.append(pass_on(modes[1], "x", AHEAD))
    last_image = pass_on(images[1], "y", AHEAD)

    turns = (0, 1, -1, 2)
    keep, send = product(place, modes, images, turns)
    received = lax.ppermute(send, "core", SWAP)
    keep_last, send_last = product(place, modes, [last_image], turns)
    received_last = lax.ppermute(send_last, "core", SWAP)
    two_first = pl.pallas_call(
        ahead_kernel,
        out_shape=jax.ShapeDtypeStruct((3, 64, 128), F32),
        in_specs=[whole, whole, anywhere],
        out_specs=whole,
        compiler_params=pltpu.CompilerParams(vmem_limit_bytes=VMEM_BYTES),
        cost_estimate=pl.CostEstimate(flops=30_000, bytes_accessed=300_000, transcendentals=0),
    )(keep, received, send_last)
    sums = (keep, received, keep_last, received_last)
    full = jax.ShapeDtypeStruct((4, 64, 128), F32)
    one = pl.pallas_call(
        next_kernel,
        out_shape=full,
        in_specs=[whole] * 4 + [anywhere],
        out_specs=whole,
        compiler_params=pltpu.CompilerParams(vmem_limit_bytes=VMEM_BYTES),
    )(*sums, two_first)
    one = near_move(one, 1)
    two_first = near_move(two_first, 2)
    own, back, two_last = pl.pallas_call(
        rest_kernel,
        out_shape=[full, full, jax.ShapeDtypeStruct((1, 64, 128), F32)],
        in_specs=[whole] * 4 + [anywhere],
        out_specs=[whole] * 3,
        compiler_params=pltpu.CompilerParams(vmem_limit_bytes=VMEM_BYTES),
    )(*sums, two_first)
    near = pl.pallas_call(
        near_kernel,
        out_shape=jax.ShapeDtypeStruct((4, 64, 128), F32),
        in_specs=[scalars] + [whole] * 5,
        out_specs=whole,
        compiler_params=pltpu.CompilerParams(vmem_limit_bytes=VMEM_BYTES),
    )(place, own, one, near_move(back, 3), two_first, near_move(two_last, 2))
    far = lax.all_to_all(near, "zh", 0, 0, tiled=True)
    piece = kernel_call(
        functools.partial(far_kernel, weight), jax.ShapeDtypeStruct((64, 128), F32), moved=200_000
    )(far)
    reduced = turn_over(piece).T
    return reduced, advected.reshape(basis.shape), r_factor


def solution(mesh):
    fine = Mesh(mesh.devices.reshape(4, 4, 2, 4, 4), AXES)
    placed = (
        P(None, SPACE, None, None, MODE),
        P(None, SPACE, None, None),
        P(None, None, SPACE, None, None),
        P(SPACE, None, None),
    )
    return jax.shard_map(
        body,
        mesh=fine,
        in_specs=placed,
        out_specs=(P(MODE, SPACE), P(None, SPACE, None, None, MODE), P(MODE, None)),
        check_vma=False,
    )
```
